32 devices in a mesh: line: 4 (over x, core), dp: 8 (over z, y).
Axes of the slice: x: 2, y: 2, z: 4, core: 2. Of those that a mesh axis runs over, the one named last changes fastest.
Arguments:
- fields: bfloat16 [8, 2048, 128], P('dp', 'line'), may hold values from -6 to 6
- cotangent: bfloat16 [8, 2048, 128], P('dp', 'line'), may hold values from -6 to 6
- norm_gain: float32 [3, 128], replicated, may hold values from 0.1 to 1.9
- kernel: float32 [3, 15, 128], replicated, may hold values from -1.8 to 1.8
- mix_weight: bfloat16 [3, 128, 128], replicated, may hold values from -0.5 to 0.5
- line_order: int32 [3, 2048], P(None, 'line'), may hold values from 0 to 511, as said below
- line_starts: int32 [3, 16], P(None, 'line'), may hold values from 0 to 32
Outputs:
- imitated: bfloat16 [8, 2048, 128], P('dp', 'line')
- field_grad: bfloat16 [8, 2048, 128], P('dp', 'line')
- mix_grad: float32 [3, 128, 128], replicated
- kernel_grad: float32 [3, 15, 128], replicated
- gain_grad: float32 [3, 128], replicated
The draws below stay inside these ranges and needn't reach their ends.
Inputs may be any that keep to these rules, and one draw needn't show every extreme that they name: For each direction, every aligned block of 512 entries of line_order is a permutation of 0 to 511.
All inputs are finite; a program needn't handle non-finite values.
Results may differ from the reference program's by a relative error of at most 0.014.
Values may be sent and summed in bfloat16 or wider, within the bound.
A program may use at most 64 MiB of HBM per device.

```python
import jax
import jax.numpy as jnp
from jax import lax

C = 128
LINE = 128
TAPS = 15
CELL_DEV = 512
SAMPLES = 8
NCELL = 2048
NLINES = 16
N_LINE = 4


def draw_line_order(key, part):
    holders = NCELL // CELL_DEV
    keys = jax.random.split(jax.random.fold_in(key, 17), 3 * holders)
    tables = jax.vmap(lambda single_key: jax.random.permutation(single_key, CELL_DEV))(keys)
    return tables.reshape(3, NCELL).astype(jnp.int32)


def with_ends(result, stream_key, smallest, largest):
    extent = result.shape
    index_at = [jax.random.randint(jax.random.fold_in(stream_key, axis), (), 0, extent[axis]) for axis in range(len(extent))]
    result = result.at[tuple(index_at)].set(smallest)
    longest = extent.index(max(extent))
    index_at[longest] = (index_at[longest] + 1) % extent[longest]
    return result.at[tuple(index_at)].set(largest)


def block_levels(key, shape, pieces, least, top_value):
    gain = 1.0
    for dim, shards_of in pieces:
        draws = jax.random.uniform(jax.random.fold_in(jax.random.fold_in(key, 6), dim), (shards_of,), jnp.float32, least / len(pieces), top_value / len(pieces))
        gain = gain * jnp.repeat(jnp.exp(draws), shape[dim] // shards_of).reshape((-1,) + (1,) * (len(shape) - 1 - dim))
    return gain


def normal_values(stream_key, shape, deviation, bound, cuts=(), held_as=jnp.bfloat16):
    loudness = block_levels(stream_key, shape, cuts, -0.22, 0.18) if cuts else 1.0
    array = jax.random.normal(stream_key, shape, jnp.float32) * deviation * loudness
    return jnp.minimum(jnp.maximum(array, -bound), bound).astype(held_as)


def setup_inputs(seed: int = 0) -> dict:
    splits = jax.random.split(jax.random.key(seed), 8)
    fields = normal_values(splits[0], (SAMPLES, NCELL, C), 1.0, 6.0, ((0, 8), (1, 4)))
    cotangent = normal_values(splits[1], (SAMPLES, NCELL, C), 1.0, 6.0, ((0, 8), (1, 4)))
    norm_gain = jnp.clip(1.0 + 0.18 * jax.random.normal(splits[2], (3, C), jnp.float32), 0.1, 1.9)
    kernel = normal_values(splits[3], (3, TAPS, C), 0.3, 1.8, (), jnp.float32)
    mix_weight = normal_values(splits[4], (3, C, C), C ** -0.5, 0.5)
    line_order = draw_line_order(jax.random.fold_in(splits[7], 71), 0)
    line_starts = with_ends(jax.random.randint(splits[6], (3, NLINES), 0, 33), jax.random.fold_in(splits[6], 1), 0, 32).astype(jnp.int32)
    return {"fields": fields, "cotangent": cotangent, "norm_gain": norm_gain, "kernel": kernel, "mix_weight": mix_weight, "line_order": line_order, "line_starts": line_starts}


EPSILON = 1e-06

def tap_offsets():
    offsets = [0]
    for dilation_level in range(7):
        offsets = offsets + [-2 ** dilation_level, 2 ** dilation_level]
    return offsets

def shifted(values, offset):
    if offset > 0:
        return jnp.concatenate([values[:, offset:], jnp.zeros_like(values[:, :offset])], axis=1)
    if offset < 0:
        return jnp.concatenate([jnp.zeros_like(values[:, offset:]), values[:, :offset]], axis=1)
    return values

def depthwise(inputs, weights):
    running = jnp.zeros(inputs.shape, jnp.float32)
    for tap_index, offset in enumerate(tap_offsets()):
        running = running + weights[tap_index] * shifted(inputs, offset)
    return running

def depthwise_transpose(grads, weights):
    running = jnp.zeros(grads.shape, jnp.float32)
    for tap_index, offset in enumerate(tap_offsets()):
        running = running + weights[tap_index] * shifted(grads, -offset)
    return running

def kernel_terms(grads, inputs):
    return jnp.stack([lax.optimization_barrier(jnp.sum(grads * shifted(inputs, offset), axis=(0, 1))) for offset in tap_offsets()])

def sources(line_order, direction):
    piece_len = CELL_DEV // N_LINE
    position = jnp.arange(NCELL, dtype=jnp.int32)
    holder = position // CELL_DEV
    entries = line_order[direction]
    anchor = entries // piece_len
    within = entries % piece_len
    blocks_at = (holder - direction * anchor) % N_LINE
    return (anchor * CELL_DEV + blocks_at * piece_len + within).astype(jnp.int32)

def keep_lines(line_starts, direction):
    position = jnp.arange(LINE, dtype=jnp.int32)
    return position[None, :] >= line_starts[direction][:, None]

def one_sample(sample, grad_out, norm_gain, kernel, mix_weight, gathers, scatters, masks):
    stream = sample
    saved = []
    for direction in range(3):
        values = stream.astype(jnp.float32)
        inverse = lax.rsqrt(lax.optimization_barrier(jnp.mean(values * values, axis=-1, keepdims=True)) + EPSILON)
        scaled = values * inverse
        normed = (scaled * norm_gain[direction]).astype(jnp.bfloat16)
        regrouped = normed[gathers[direction]].reshape(NLINES, LINE, C)
        masked = jnp.where(masks[direction][:, :, None], regrouped, jnp.zeros_like(regrouped))
        hidden = depthwise(masked.astype(jnp.float32), kernel[direction])
        activated = jax.nn.silu(hidden).astype(jnp.bfloat16)
        mixed = jnp.dot(activated.reshape(NCELL, C), mix_weight[direction], preferred_element_type=jnp.float32).astype(jnp.bfloat16)
        stream = (values + mixed[scatters[direction]].astype(jnp.float32)).astype(jnp.bfloat16)
        saved.append((inverse, scaled, masked, hidden, activated))
    grad_stream = grad_out
    mix_list = [None, None, None]
    kernel_list = [None, None, None]
    gain_list = [None, None, None]
    for direction in (2, 1, 0):
        inverse, scaled, masked, hidden, activated = saved[direction]
        grad_mixed = grad_stream[gathers[direction]]
        mix_list[direction] = jnp.dot(activated.reshape(NCELL, C).T, grad_mixed, preferred_element_type=jnp.float32)
        grad_act = jnp.dot(grad_mixed, mix_weight[direction].T, preferred_element_type=jnp.float32).reshape(NLINES, LINE, C)
        gate_value = jax.nn.sigmoid(hidden)
        grad_hidden = (grad_act * (gate_value * (1.0 + hidden * (1.0 - gate_value)))).astype(jnp.bfloat16)
        hidden_grad_f = grad_hidden.astype(jnp.float32)
        kernel_list[direction] = kernel_terms(hidden_grad_f, masked.astype(jnp.float32))
        grad_masked = depthwise_transpose(hidden_grad_f, kernel[direction])
        grad_normed = jnp.where(masks[direction][:, :, None], grad_masked, jnp.zeros_like(grad_masked)).astype(jnp.bfloat16)
        grad_cells = grad_normed.reshape(NCELL, C)[scatters[direction]].astype(jnp.float32)
        gain_list[direction] = lax.optimization_barrier(jnp.sum(grad_cells * scaled, axis=0))
        weighted = grad_cells * norm_gain[direction]
        grad_norm = inverse * (weighted - scaled * lax.optimization_barrier(jnp.mean(weighted * scaled, axis=-1, keepdims=True)))
        grad_stream = (grad_stream.astype(jnp.float32) + grad_norm).astype(jnp.bfloat16)
    return (stream, grad_stream, jnp.stack(mix_list), jnp.stack(kernel_list), jnp.stack(gain_list))

def reference(fields, cotangent, norm_gain, kernel, mix_weight, line_order, line_starts):
    gathers = [sources(line_order, direction) for direction in range(3)]
    scatters = [jnp.zeros((NCELL,), jnp.int32).at[gathers[direction]].set(jnp.arange(NCELL, dtype=jnp.int32)) for direction in range(3)]
    masks = [keep_lines(line_starts, direction) for direction in range(3)]

    def run_sample(sample_pair):
        return one_sample(sample_pair[0], sample_pair[1], norm_gain, kernel, mix_weight, gathers, scatters, masks)
    imitated, field_grad, mix_parts, kernel_parts, gain_parts = lax.map(run_sample, (fields, cotangent))
    grad_scale = float(SAMPLES * NCELL) ** (-0.5)
    mix_grad = lax.optimization_barrier(jnp.sum(mix_parts, axis=0)) * grad_scale
    kernel_grad = lax.optimization_barrier(jnp.sum(kernel_parts, axis=0)) * grad_scale
    gain_grad = lax.optimization_barrier(jnp.sum(gain_parts, axis=0)) * grad_scale
    return (imitated, field_grad, mix_grad, kernel_grad, gain_grad)
```

```python
import functools

import jax
import jax.numpy as jnp
from jax import lax
from jax.experimental import pallas as pl
from jax.experimental.pallas import tpu as pltpu
from jax.sharding import PartitionSpec as P

EPSILON = 1e-06
EDGE = 8
F32 = jnp.float32
BF16 = jnp.bfloat16


def tap_offsets(taps):
    offsets = [0]
    for dilation_level in range((taps - 1) // 2):
        offsets = offsets + [-(2**dilation_level), 2**dilation_level]
    return offsets


def fold(values):
    return jnp.sum(values.reshape(-1, 8, values.shape[1]), axis=0)


def kernel_body(
    shape,
    fields,
    cotangent,
    gain_ref,
    taps_ref,
    mix_ref,
    order_ref,
    starts_ref,
    imitated,
    field_grad,
    mix_out,
    taps_out,
    gain_out,
    gather,
    scatter,
    recv,
    placed,
    stream,
    scaled,
    inverse,
    masked,
    slope,
    activated,
    grads,
    padded,
    sums,
    parts,
    a_recv,
    b_recv,
    full,
    ex_send,
    ex_recv,
    a_send,
    a_arrive,
    b_send,
    b_arrive,
    c_send,
    c_arrive,
    local_sem,
):
    ranks, copies, line_len, scale = shape
    cells, channels = stream.shape
    lines = cells // line_len
    block = cells // ranks
    taps = taps_ref.shape[1]
    offsets = tap_offsets(taps)
    piece = parts.shape[1] // ranks
    me = lax.axis_index("line")
    my_dp = lax.axis_index("dp")

    def peer(step):
        return lax.rem(me + step, ranks)

    def dp_peer(step):
        return lax.rem(my_dp + step, copies)

    def rows(index, size):
        return pl.ds(pl.multiple_of(index * size, size), size)

    barrier = pltpu.get_barrier_semaphore()
    for step in range(1, ranks):
        pl.semaphore_signal(
            barrier, inc=1, device_id={"line": peer(step)}, device_id_type=pl.DeviceIdType.MESH
        )
    for step in range(1, copies):
        pl.semaphore_signal(
            barrier, inc=1, device_id={"dp": dp_peer(step)}, device_id_type=pl.DeviceIdType.MESH
        )
    pl.semaphore_wait(barrier, ranks - 1 + copies - 1)

    unsent = []

    def send(stage, step, source, target):
        copy = pltpu.make_async_remote_copy(
            src_ref=source,
            dst_ref=target,
            send_sem=ex_send.at[stage, step],
            recv_sem=ex_recv.at[stage, step],
            device_id={"line": peer(step)},
            device_id_type=pl.DeviceIdType.MESH,
        )
        copy.start()
        unsent.append(copy)
        return copy

    def enter(stage, array, shift):
        out = []
        for step in range(1, ranks):
            chunk = lax.rem(peer(step) + ranks * shift - shift * me, ranks)
            out.append(
                send(stage, step, array.at[0, rows(chunk, block)], recv.at[stage, rows(me, block)])
            )
        chunk = lax.rem(me + ranks * shift - shift * me, ranks)
        own = pltpu.make_async_copy(
            array.at[0, rows(chunk, block)], recv.at[stage, rows(me, block)], local_sem.at[stage]
        )
        own.start()
        return out, own

    arriving, own_fields = enter(0, fields, 0)

    def tables(direction):
        row = order_ref[direction : direction + 1, :]
        lanes = 128
        across = lax.broadcasted_iota(jnp.int32, (cells, cells), 0)
        scatter[direction] = jnp.where(across == row, 1.0, 0.0).astype(BF16)
        turned = jnp.transpose(jnp.broadcast_to(row, (lanes, cells)))
        for first in range(0, cells, lanes):
            width = lax.broadcasted_iota(jnp.int32, (cells, lanes), 1) + first
            gather[direction, :, first : first + lanes] = jnp.where(
                turned == width, 1.0, 0.0
            ).astype(BF16)

    tables(0)
    padded[...] = jnp.zeros_like(padded)
    parts[...] = jnp.zeros_like(parts)

    def hand_over(stage, direction, values, sign):
        out = []
        for anchor in list(range(1, ranks)) + [0]:
            span = pl.ds(anchor * block, block)
            chunk = jnp.dot(
                scatter[direction, span, :], values, preferred_element_type=F32
            ).astype(BF16)
            if anchor:
                placed[stage, span, :] = chunk
                step = (sign * anchor) % ranks
                out.append(send(stage, step, placed.at[stage, span], recv.at[stage, span]))
            else:
                recv[stage, span, :] = chunk
        return out

    def leave(stage, direction, values, target):
        chunk = jnp.dot(scatter[direction], values, preferred_element_type=F32)
        placed[stage] = chunk.astype(BF16)
        out = []
        for step in range(1, ranks):
            anchor = peer(step)
            where = lax.rem(me + direction * (ranks - anchor), ranks)
            out.append(
                send(
                    stage, step, placed.at[stage, rows(anchor, block)],
                    target.at[0, rows(where, block)],
                )
            )
        where = lax.rem(me + direction * (ranks - me), ranks)
        own = pltpu.make_async_copy(
            placed.at[stage, rows(me, block)], target.at[0, rows(where, block)],
            local_sem.at[stage],
        )
        own.start()
        return out, own

    def take(stage, direction, copies_in):
        for copy in copies_in:
            copy.wait_recv()
        return jnp.dot(gather[direction], recv[stage], preferred_element_type=F32)

    def keep_rows(direction, line):
        position = lax.broadcasted_iota(jnp.int32, (line_len, channels), 0)
        return position >= starts_ref[direction, line]

    def forward(direction):
        def one_line(line, carry):
            here = rows(line, line_len)
            values = stream[here, :]
            norm = lax.rsqrt(jnp.mean(values * values, axis=-1, keepdims=True) + EPSILON)
            ratio = values * norm
            normed = (ratio * gain_ref[direction : direction + 1, :]).astype(BF16).astype(F32)
            inputs = jnp.where(keep_rows(direction, line), normed, 0.0)
            padded[pl.ds(EDGE, line_len), :] = inputs
            inverse[direction, here, :] = jnp.broadcast_to(norm, (line_len, channels))
            scaled[direction, here, :] = ratio
            masked[direction, here, :] = inputs
            hidden = taps_ref[direction, 0:1, :] * inputs
            for tap in range(1, taps):
                offset = offsets[tap]
                weight = taps_ref[direction, tap : tap + 1, :]
                size = abs(offset)
                if size < EDGE:
                    hidden = hidden + weight * padded[pl.ds(EDGE + offset, line_len), :]
                elif offset > 0:
                    inner = hidden[: line_len - size] + weight * inputs[size:]
                    hidden = jnp.concatenate([inner, hidden[line_len - size :]], axis=0)
                else:
                    inner = hidden[size:] + weight * inputs[: line_len - size]
                    hidden = jnp.concatenate([hidden[:size], inner], axis=0)
            gate = 0.5 * jnp.tanh(0.5 * hidden) + 0.5
            activated[direction, here, :] = (hidden * gate).astype(BF16)
            slope[direction, here, :] = gate * (1.0 + hidden * (1.0 - gate))
            return carry

        lax.fori_loop(0, lines, one_line, 0)
        mixed = jnp.dot(activated[direction], mix_ref[direction], preferred_element_type=F32)
        return (stream[...] + mixed.astype(BF16).astype(F32)).astype(BF16)

    own_fields.wait()
    stream[...] = take(0, 0, arriving)
    cot_arriving, own_cot = enter(1, cotangent, 2)
    moved = forward(0)
    arriving = hand_over(2, 0, moved, 1)
    tables(1)
    stream[...] = take(2, 1, arriving)
    moved = forward(1)
    arriving = hand_over(3, 1, moved, 1)
    tables(2)
    stream[...] = take(3, 2, arriving)
    moved = forward(2)
    out_arriving, own_out = leave(4, 2, moved, imitated)
    own_cot.wait()
    grads[...] = take(1, 2, cot_arriving)

    def backward(direction):
        grad_mixed = grads[...].astype(BF16)
        parts[direction, :channels, :] = lax.dot_general(
            activated[direction], grad_mixed, (((0,), (0,)), ((), ())), preferred_element_type=F32
        )
        stream[...] = lax.dot_general(
            grad_mixed, mix_ref[direction], (((1,), (1,)), ((), ())), preferred_element_type=F32
        )
        sums[...] = jnp.zeros_like(sums)

        def one_line(line, carry):
            here = rows(line, line_len)
            grad = (stream[here, :] * slope[direction, here, :]).astype(BF16).astype(F32)
            padded[pl.ds(EDGE, line_len), :] = grad
            inputs = masked[direction, here, :]
            total = taps_ref[direction, 0:1, :] * grad
            sums[0:8, :] += fold(grad * inputs)
            for tap in range(1, taps):
                offset = -offsets[tap]
                weight = taps_ref[direction, tap : tap + 1, :]
                size = abs(offset)
                slot = pl.ds(8 * tap, 8)
                if size < EDGE:
                    near = padded[pl.ds(EDGE + offset, line_len), :]
                    total = total + weight * near
                    sums[slot, :] += fold(near * inputs)
                elif offset > 0:
                    near = grad[size:]
                    inner = total[: line_len - size] + weight * near
                    total = jnp.concatenate([inner, total[line_len - size :]], axis=0)
                    sums[slot, :] += fold(near * inputs[: line_len - size])
                else:
                    near = grad[: line_len - size]
                    inner = total[size:] + weight * near
                    total = jnp.concatenate([total[:size], inner], axis=0)
                    sums[slot, :] += fold(near * inputs[size:])
            cell = jnp.where(keep_rows(direction, line), total, 0.0).astype(BF16).astype(F32)
            ratio = scaled[direction, here, :]
            sums[8 * taps : 8 * taps + 8, :] += fold(cell * ratio)
            weighted = cell * gain_ref[direction : direction + 1, :]
            centre = jnp.mean(weighted * ratio, axis=-1, keepdims=True)
            change = inverse[direction, here, :] * (weighted - ratio * centre)
            grads[here, :] = grads[here, :] + change
            return carry

        lax.fori_loop(0, lines, one_line, 0)
        parts[direction, channels : channels + taps + 1, :] = jnp.sum(
            sums[...].reshape(taps + 1, 8, channels), axis=1
        )
        return grads[...].astype(BF16)

    def reduce_line(direction):
        out = []
        for step in range(1, ranks):
            copy = pltpu.make_async_remote_copy(
                src_ref=parts.at[direction, rows(peer(step), piece)],
                dst_ref=a_recv.at[direction, step],
                send_sem=a_send.at[direction, step],
                recv_sem=a_arrive.at[direction, step],
                device_id={"line": peer(step)},
                device_id_type=pl.DeviceIdType.MESH,
            )
            copy.start()
            unsent.append(copy)
            out.append(copy)
        return out

    def reduce_dp(direction, copies_in):
        total = parts[direction, rows(me, piece), :]
        for step in range(1, ranks):
            copies_in[step - 1].wait_recv()
            total = total + a_recv[direction, step]
        b_recv[direction, my_dp] = total
        out = []
        for step in range(1, copies):
            copy = pltpu.make_async_remote_copy(
                src_ref=b_recv.at[direction, my_dp],
                dst_ref=b_recv.at[direction, my_dp],
                send_sem=b_send.at[direction, step],
                recv_sem=b_arrive.at[direction, step],
                device_id={"dp": dp_peer(step)},
                device_id_type=pl.DeviceIdType.MESH,
            )
            copy.start()
            unsent.append(copy)
            out.append(copy)
        return out

    def spread(direction, copies_in):
        for copy in copies_in:
            copy.wait_recv()
        total = b_recv[direction, 0]
        for index in range(1, copies):
            total = total + b_recv[direction, index]
        full[direction, rows(me, piece), :] = total * scale
        out = []
        for step in range(1, ranks):
            copy = pltpu.make_async_remote_copy(
                src_ref=full.at[direction, rows(me, piece)],
                dst_ref=full.at[direction, rows(me, piece)],
                send_sem=c_send.at[direction, step],
                recv_sem=c_arrive.at[direction, step],
                device_id={"line": peer(step)},
                device_id_type=pl.DeviceIdType.MESH,
            )
            copy.start()
            unsent.append(copy)
            out.append(copy)
        return out

    def finish(direction, copies_in):
        for copy in copies_in:
            copy.wait_recv()
        mix_out[direction] = full[direction, :channels, :]
        taps_out[direction] = full[direction, channels : channels + taps, :]
        gain_out[direction : direction + 1, :] = full[
            direction, channels + taps : channels + taps + 1, :
        ]

    moved = backward(2)
    arriving = hand_over(5, 2, moved, -1)
    a2 = reduce_line(2)
    grads[...] = take(5, 1, arriving)
    moved = backward(1)
    arriving = hand_over(6, 1, moved, -1)
    a1 = reduce_line(1)
    b2 = reduce_dp(2, a2)
    grads[...] = take(6, 0, arriving)
    moved = backward(0)
    a0 = reduce_line(0)
    last_arriving, own_last = leave(7, 0, moved, field_grad)
    b1 = reduce_dp(1, a1)
    c2 = spread(2, b2)
    b0 = reduce_dp(0, a0)
    c1 = spread(1, b1)
    finish(2, c2)
    c0 = spread(0, b0)
    finish(1, c1)
    finish(0, c0)
    for copy in out_arriving + last_arriving:
        copy.wait_recv()
    own_out.wait()
    own_last.wait()
    for copy in unsent:
        copy.wait_send()


def body(fields, cotangent, norm_gain, kernel, mix_weight, line_order, line_starts):
    ranks = lax.axis_size("line")
    copies = lax.axis_size("dp")
    batch, cells, channels = fields.shape
    assert batch == 1
    directions, taps = kernel.shape[:2]
    line_len = cells // line_starts.shape[1]
    scale = float(copies * batch * ranks * cells) ** (-0.5)
    unit = 8 * ranks
    part_rows = -(-(channels + taps + 1) // unit) * unit
    piece = part_rows // ranks
    stages = 2 * directions + 2
    vmem = pl.BlockSpec(memory_space=pltpu.VMEM)
    smem = pl.BlockSpec(memory_space=pltpu.SMEM)
    anywhere = pl.BlockSpec(memory_space=pl.ANY)
    wide = pltpu.VMEM((directions, cells, channels), F32)
    dma = pltpu.SemaphoreType.DMA
    return pl.pallas_call(
        functools.partial(kernel_body, (ranks, copies, line_len, scale)),
        out_shape=(
            jax.ShapeDtypeStruct(fields.shape, BF16),
            jax.ShapeDtypeStruct(fields.shape, BF16),
            jax.ShapeDtypeStruct((directions, channels, channels), F32),
            jax.ShapeDtypeStruct((directions, taps, channels), F32),
            jax.ShapeDtypeStruct((directions, channels), F32),
        ),
        in_specs=[anywhere, anywhere, vmem, vmem, vmem, vmem, smem],
        out_specs=(anywhere, anywhere, vmem, vmem, vmem),
        scratch_shapes=[
            pltpu.VMEM((directions, cells, cells), BF16),
            pltpu.VMEM((directions, cells, cells), BF16),
            pltpu.VMEM((stages, cells, channels), BF16),
            pltpu.VMEM((stages, cells, channels), BF16),
            pltpu.VMEM((cells, channels), F32),
            wide,
            wide,
            wide,
            wide,
            pltpu.VMEM((directions, cells, channels), BF16),
            pltpu.VMEM((cells, channels), F32),
            pltpu.VMEM((line_len + 2 * EDGE, channels), F32),
            pltpu.VMEM(((taps + 1) * 8, channels), F32),
            pltpu.VMEM((directions, part_rows, channels), F32),
            pltpu.VMEM((directions, ranks, piece, channels), F32),
            pltpu.VMEM((directions, copies, piece, channels), F32),
            pltpu.VMEM((directions, part_rows, channels), F32),
            dma((stages, ranks)),
            dma((stages, ranks)),
            dma((directions, ranks)),
            dma((directions, ranks)),
            dma((directions, copies)),
            dma((directions, copies)),
            dma((directions, ranks)),
            dma((directions, ranks)),
            dma((stages,)),
        ],
        compiler_params=pltpu.CompilerParams(
            collective_id=0, has_side_effects=True, vmem_limit_bytes=40 * 1024 * 1024
        ),
        name="mesh_block",
    )(fields, cotangent, norm_gain, kernel, mix_weight, line_order, line_starts)


def solution(mesh):
    in_specs = (
        P("dp", "line", None),
        P("dp", "line", None),
        P(),
        P(),
        P(),
        P(None, "line"),
        P(None, "line"),
    )
    out_specs = (P("dp", "line", None), P("dp", "line", None), P(), P(), P())
    return jax.shard_map(body, mesh=mesh, in_specs=in_specs, out_specs=out_specs, check_vma=False)
```

```python
import functools

import jax
import jax.numpy as jnp
from jax import lax
from jax.experimental import pallas as pl
from jax.experimental.pallas import tpu as pltpu
from jax.sharding import PartitionSpec as P

EPSILON = 1e-06
EDGE = 8
F32 = jnp.float32
BF16 = jnp.bfloat16


def tap_offsets(taps):
    offsets = [0]
    for dilation_level in range((taps - 1) // 2):
        offsets = offsets + [-(2**dilation_level), 2**dilation_level]
    return offsets


def fold(values):
    return jnp.sum(values.reshape(-1, 8, values.shape[1]), axis=0)


def kernel_body(
    shape,
    fields,
    cotangent,
    gain_hbm,
    taps_hbm,
    mix_hbm,
    order_hbm,
    starts_hbm,
    imitated,
    field_grad,
    mix_out,
    taps_out,
    gain_out,
    gain_ref,
    taps_ref,
    mix_ref,
    order_ref,
    starts_ref,
    gather,
    scatter,
    recv,
    placed,
    stream,
    scaled,
    inverse,
    masked,
    slope,
    activated,
    grads,
    padded,
    sums,
    parts,
    a_recv,
    b_recv,
    full,
    line_tails,
    dp_tails,
    ex_send,
    ex_recv,
    a_send,
    a_arrive,
    b_send,
    b_arrive,
    c_send,
    c_arrive,
    t_send,
    t_arrive,
    u_send,
    u_arrive,
    local_sem,
    load_sem,
):
    ranks, copies, line_len, scale = shape
    cells, channels = stream.shape
    lines = cells // line_len
    block = cells // ranks
    taps = taps_ref.shape[1]
    offsets = tap_offsets(taps)
    piece = parts.shape[1] // ranks
    me = lax.axis_index("line")
    my_dp = lax.axis_index("dp")

    loads = []
    for index, (source, target) in enumerate(
        (
            (order_hbm, order_ref),
            (gain_hbm, gain_ref),
            (taps_hbm, taps_ref),
            (starts_hbm, starts_ref),
            (mix_hbm, mix_ref),
        )
    ):
        load = pltpu.make_async_copy(source, target, load_sem.at[index])
        load.start()
        loads.append(load)

    def peer(step):
        return lax.rem(me + step, ranks)

    def dp_peer(step):
        return lax.rem(my_dp + step, copies)

    def rows(index, size):
        return pl.ds(pl.multiple_of(index * size, size), size)

    barrier = pltpu.get_barrier_semaphore()
    for step in range(1, ranks):
        pl.semaphore_signal(
            barrier, inc=1, device_id={"line": peer(step)}, device_id_type=pl.DeviceIdType.MESH
        )
    for step in range(1, copies):
        pl.semaphore_signal(
            barrier, inc=1, device_id={"dp": dp_peer(step)}, device_id_type=pl.DeviceIdType.MESH
        )
    pl.semaphore_wait(barrier, ranks - 1 + copies - 1)

    unsent = []

    def remote(source, target, send_sem, recv_sem, where):
        copy = pltpu.make_async_remote_copy(
            src_ref=source,
            dst_ref=target,
            send_sem=send_sem,
            recv_sem=recv_sem,
            device_id=where,
            device_id_type=pl.DeviceIdType.MESH,
        )
        copy.start()
        unsent.append(copy)
        return copy

    def send(stage, step, source, target):
        return remote(
            source, target, ex_send.at[stage, step], ex_recv.at[stage, step], {"line": peer(step)}
        )

    def enter(stage, array, shift):
        out = []
        for step in range(1, ranks):
            chunk = lax.rem(peer(step) + ranks * shift - shift * me, ranks)
            out.append(
                send(stage, step, array.at[0, rows(chunk, block)], recv.at[stage, rows(me, block)])
            )
        chunk = lax.rem(me + ranks * shift - shift * me, ranks)
        own = pltpu.make_async_copy(
            array.at[0, rows(chunk, block)], recv.at[stage, rows(me, block)], local_sem.at[stage]
        )
        own.start()
        return out, own

    arriving, own_fields = enter(0, fields, 0)

    def tables(direction):
        row = order_ref[direction : direction + 1, :]
        lanes = 128
        across = lax.broadcasted_iota(jnp.int32, (cells, cells), 0)
        scatter[direction] = jnp.where(across == row, 1.0, 0.0).astype(BF16)
        turned = jnp.transpose(jnp.broadcast_to(row, (lanes, cells)))
        for first in range(0, cells, lanes):
            width = lax.broadcasted_iota(jnp.int32, (cells, lanes), 1) + first
            gather[direction, :, first : first + lanes] = jnp.where(
                turned == width, 1.0, 0.0
            ).astype(BF16)

    masked[...] = jnp.zeros_like(masked)
    padded[...] = jnp.zeros_like(padded)
    for load in loads:
        load.wait()
    tables(0)

    def hand_over(stage, direction, values, sign):
        out = []
        for anchor in list(range(1, ranks)) + [0]:
            span = pl.ds(anchor * block, block)
            chunk = jnp.dot(
                scatter[direction, span, :], values, preferred_element_type=F32
            ).astype(BF16)
            if anchor:
                placed[stage, span, :] = chunk
                step = (sign * anchor) % ranks
                out.append(send(stage, step, placed.at[stage, span], recv.at[stage, span]))
            else:
                recv[stage, span, :] = chunk
        return out

    def leave(stage, direction, values, target):
        chunk = jnp.dot(scatter[direction], values, preferred_element_type=F32)
        placed[stage] = chunk.astype(BF16)
        out = []
        for step in range(1, ranks):
            anchor = peer(step)
            where = lax.rem(me + direction * (ranks - anchor), ranks)
            out.append(
                send(
                    stage,
                    step,
                    placed.at[stage, rows(anchor, block)],
                    target.at[0, rows(where, block)],
                )
            )
        where = lax.rem(me + direction * (ranks - me), ranks)
        own = pltpu.make_async_copy(
            placed.at[stage, rows(me, block)],
            target.at[0, rows(where, block)],
            local_sem.at[stage],
        )
        own.start()
        return out, own

    def take(stage, direction, copies_in):
        for copy in copies_in:
            copy.wait_recv()
        return jnp.dot(gather[direction], recv[stage], preferred_element_type=F32)

    def keep_rows(direction, line):
        position = lax.broadcasted_iota(jnp.int32, (line_len, channels), 0)
        return position >= starts_ref[direction : direction + 1, line : line + 1]

    inside = pl.ds(EDGE, line_len)

    def forward(direction):
        for line in range(lines):
            here = pl.ds(line * line_len, line_len)
            values = stream[here, :]
            norm = lax.rsqrt(jnp.mean(values * values, axis=-1, keepdims=True) + EPSILON)
            ratio = values * norm
            normed = (ratio * gain_ref[direction : direction + 1, :]).astype(BF16).astype(F32)
            masked[direction, line, inside, :] = jnp.where(keep_rows(direction, line), normed, 0.0)
            inverse[direction, here, :] = jnp.broadcast_to(norm, (line_len, channels))
            scaled[direction, here, :] = ratio

        def one_line(line, carry):
            here = rows(line, line_len)
            inputs = masked[direction, line, inside, :]
            hidden = taps_ref[direction, 0:1, :] * inputs
            for tap in range(1, taps):
                offset = offsets[tap]
                weight = taps_ref[direction, tap : tap + 1, :]
                size = abs(offset)
                if size < EDGE:
                    near = masked[direction, line, pl.ds(EDGE + offset, line_len), :]
                    hidden = hidden + weight * near
                elif offset > 0:
                    inner = hidden[: line_len - size] + weight * inputs[size:]
                    hidden = jnp.concatenate([inner, hidden[line_len - size :]], axis=0)
                else:
                    inner = hidden[size:] + weight * inputs[: line_len - size]
                    hidden = jnp.concatenate([hidden[:size], inner], axis=0)
            gate = 0.5 * jnp.tanh(0.5 * hidden) + 0.5
            activated[direction, here, :] = (hidden * gate).astype(BF16)
            slope[direction, here, :] = gate * (1.0 + hidden * (1.0 - gate))
            return carry

        lax.fori_loop(0, lines, one_line, 0)
        mixed = jnp.dot(activated[direction], mix_ref[direction], preferred_element_type=F32)
        return (stream[...] + mixed.astype(BF16).astype(F32)).astype(BF16)

    own_fields.wait()
    stream[...] = take(0, 0, arriving)
    cot_arriving, own_cot = enter(1, cotangent, 2)
    moved = forward(0)
    arriving = hand_over(2, 0, moved, 1)
    tables(1)
    stream[...] = take(2, 1, arriving)
    moved = forward(1)
    arriving = hand_over(3, 1, moved, 1)
    tables(2)
    stream[...] = take(3, 2, arriving)
    moved = forward(2)
    out_arriving, own_out = leave(4, 2, moved, imitated)
    own_cot.wait()
    grads[...] = take(1, 2, cot_arriving)

    def backward(direction):
        back = lax.dot_general(
            grads[...].astype(BF16),
            mix_ref[direction],
            (((1,), (1,)), ((), ())),
            preferred_element_type=F32,
        )
        for line in range(lines):
            here = pl.ds(line * line_len, line_len)
            local = back[line * line_len : (line + 1) * line_len] * slope[direction, here, :]
            padded[direction, line, inside, :] = local.astype(BF16).astype(F32)

        def one_line(line, carry):
            grad = padded[direction, line, inside, :]
            total = taps_ref[direction, 0:1, :] * grad
            for tap in range(1, taps):
                offset = -offsets[tap]
                weight = taps_ref[direction, tap : tap + 1, :]
                size = abs(offset)
                if size < EDGE:
                    near = padded[direction, line, pl.ds(EDGE + offset, line_len), :]
                    total = total + weight * near
                elif offset > 0:
                    inner = total[: line_len - size] + weight * grad[size:]
                    total = jnp.concatenate([inner, total[line_len - size :]], axis=0)
                else:
                    inner = total[size:] + weight * grad[: line_len - size]
                    total = jnp.concatenate([total[:size], inner], axis=0)
            stream[rows(line, line_len), :] = total
            return carry

        lax.fori_loop(0, lines, one_line, 0)
        out = []
        gains = jnp.zeros((8, channels), F32)
        for line in range(lines):
            here = pl.ds(line * line_len, line_len)
            total = jnp.where(keep_rows(direction, line), stream[here, :], 0.0)
            cell = total.astype(BF16).astype(F32)
            ratio = scaled[direction, here, :]
            gains = gains + fold(cell * ratio)
            weighted = cell * gain_ref[direction : direction + 1, :]
            centre = jnp.mean(weighted * ratio, axis=-1, keepdims=True)
            change = inverse[direction, here, :] * (weighted - ratio * centre)
            out.append((grads[here, :] + change).astype(BF16))
        sums[8 * taps : 8 * taps + 8, :] = gains
        return jnp.concatenate(out, axis=0)

    def tap_sums(direction):
        sums[0 : 8 * taps, :] = jnp.zeros((8 * taps, channels), F32)

        def one_line(line, carry):
            grad = padded[direction, line, inside, :]
            inputs = masked[direction, line, inside, :]
            for tap in range(taps):
                offset = -offsets[tap]
                size = abs(offset)
                slot = pl.ds(8 * tap, 8)
                if size == 0:
                    term = grad * inputs
                elif size < EDGE:
                    term = padded[direction, line, pl.ds(EDGE + offset, line_len), :] * inputs
                elif offset > 0:
                    term = grad[size:] * inputs[: line_len - size]
                else:
                    term = grad[: line_len - size] * inputs[size:]
                sums[slot, :] += fold(term)
            return carry

        lax.fori_loop(0, lines, one_line, 0)

    def mix_line(direction, grad_mixed):
        parts[direction] = lax.dot_general(
            activated[direction], grad_mixed, (((0,), (0,)), ((), ())), preferred_element_type=F32
        ).astype(BF16)
        return [
            remote(
                parts.at[direction, rows(peer(step), piece)],
                a_recv.at[direction, step],
                a_send.at[direction, step],
                a_arrive.at[direction, step],
                {"line": peer(step)},
            )
            for step in range(1, ranks)
        ]

    def mix_dp(direction, copies_in):
        total = parts[direction, rows(me, piece), :].astype(F32)
        for step in range(1, ranks):
            copies_in[step - 1].wait_recv()
            total = total + a_recv[direction, step].astype(F32)
        b_recv[direction, my_dp] = total.astype(BF16)
        return [
            remote(
                b_recv.at[direction, my_dp],
                b_recv.at[direction, my_dp],
                b_send.at[direction, step],
                b_arrive.at[direction, step],
                {"dp": dp_peer(step)},
            )
            for step in range(1, copies)
        ]

    def mix_spread(direction, copies_in):
        for copy in copies_in:
            copy.wait_recv()
        total = b_recv[direction, 0].astype(F32)
        for index in range(1, copies):
            total = total + b_recv[direction, index].astype(F32)
        full[direction, rows(me, piece), :] = (total * scale).astype(BF16)
        return [
            remote(
                full.at[direction, rows(me, piece)],
                full.at[direction, rows(me, piece)],
                c_send.at[direction, step],
                c_arrive.at[direction, step],
                {"line": peer(step)},
            )
            for step in range(1, ranks)
        ]

    def mix_finish(direction, copies_in):
        for copy in copies_in:
            copy.wait_recv()
        mix_out[direction] = full[direction].astype(F32)

    def tail_line(direction):
        line_tails[direction, me] = jnp.sum(sums[...].reshape(taps + 1, 8, channels), axis=1)
        return [
            remote(
                line_tails.at[direction, me],
                line_tails.at[direction, me],
                t_send.at[direction, step],
                t_arrive.at[direction, step],
                {"line": peer(step)},
            )
            for step in range(1, ranks)
        ]

    def tail_dp(direction, copies_in):
        for copy in copies_in:
            copy.wait_recv()
        total = line_tails[direction, 0]
        for index in range(1, ranks):
            total = total + line_tails[direction, index]
        dp_tails[direction, my_dp] = total
        return [
            remote(
                dp_tails.at[direction, my_dp],
                dp_tails.at[direction, my_dp],
                u_send.at[direction, step],
                u_arrive.at[direction, step],
                {"dp": dp_peer(step)},
            )
            for step in range(1, copies)
        ]

    def tail_finish(direction, copies_in):
        for copy in copies_in:
            copy.wait_recv()
        total = dp_tails[direction, 0]
        for index in range(1, copies):
            total = total + dp_tails[direction, index]
        total = total * scale
        taps_out[direction] = total[:taps]
        gain_out[direction : direction + 1, :] = total[taps : taps + 1]

    moved = backward(2)
    arriving = hand_over(5, 2, moved, -1)
    a2 = mix_line(2, grads[...].astype(BF16))
    tap_sums(2)
    t2 = tail_line(2)
    grads[...] = take(5, 1, arriving)
    moved = backward(1)
    arriving = hand_over(6, 1, moved, -1)
    b2 = mix_dp(2, a2)
    a1 = mix_line(1, grads[...].astype(BF16))
    tap_sums(1)
    t1 = tail_line(1)
    u2 = tail_dp(2, t2)
    grads[...] = take(6, 0, arriving)
    a0 = mix_line(0, grads[...].astype(BF16))
    b1 = mix_dp(1, a1)
    moved = backward(0)
    b0 = mix_dp(0, a0)
    last_arriving, own_last = leave(7, 0, moved, field_grad)
    tap_sums(0)
    t0 = tail_line(0)
    c2 = mix_spread(2, b2)
    c1 = mix_spread(1, b1)
    u1 = tail_dp(1, t1)
    u0 = tail_dp(0, t0)
    c0 = mix_spread(0, b0)
    tail_finish(2, u2)
    mix_finish(2, c2)
    mix_finish(1, c1)
    tail_finish(1, u1)
    mix_finish(0, c0)
    tail_finish(0, u0)
    for copy in out_arriving + last_arriving:
        copy.wait_recv()
    own_out.wait()
    own_last.wait()
    for copy in unsent:
        copy.wait_send()


def write_out(*refs):
    half = (len(refs) - 1) // 2
    sem = refs[-1]
    moves = [
        pltpu.make_async_copy(refs[index], refs[half + index], sem.at[index])
        for index in range(half)
    ]
    for move in moves:
        move.start()
    for move in moves:
        move.wait()


def body(fields, cotangent, norm_gain, kernel, mix_weight, line_order, line_starts):
    ranks = lax.axis_size("line")
    copies = lax.axis_size("dp")
    batch, cells, channels = fields.shape
    assert batch == 1
    directions, taps = kernel.shape[:2]
    lines = line_starts.shape[1]
    line_len = cells // lines
    scale = float(copies * batch * ranks * cells) ** (-0.5)
    piece = channels // ranks
    stages = 2 * directions + 2
    vmem = pl.BlockSpec(memory_space=pltpu.VMEM)
    hbm = pl.BlockSpec(memory_space=pltpu.HBM)
    anywhere = pl.BlockSpec(memory_space=pl.ANY)
    wide = pltpu.VMEM((directions, cells, channels), F32)
    edged = pltpu.VMEM((directions, lines, line_len + 2 * EDGE, channels), F32)
    dma = pltpu.SemaphoreType.DMA
    outs = (
        jax.ShapeDtypeStruct(fields.shape, BF16),
        jax.ShapeDtypeStruct(fields.shape, BF16),
        jax.ShapeDtypeStruct((directions, channels, channels), F32),
        jax.ShapeDtypeStruct((directions, taps, channels), F32),
        jax.ShapeDtypeStruct((directions, channels), F32),
    )
    results = pl.pallas_call(
        functools.partial(kernel_body, (ranks, copies, line_len, scale)),
        out_shape=outs,
        in_specs=[hbm] * 7,
        out_specs=(anywhere, anywhere, vmem, vmem, vmem),
        scratch_shapes=[
            pltpu.VMEM(norm_gain.shape, F32),
            pltpu.VMEM(kernel.shape, F32),
            pltpu.VMEM(mix_weight.shape, BF16),
            pltpu.VMEM(line_order.shape, jnp.int32),
            pltpu.VMEM(line_starts.shape, jnp.int32),
            pltpu.VMEM((directions, cells, cells), BF16),
            pltpu.VMEM((directions, cells, cells), BF16),
            pltpu.VMEM((stages, cells, channels), BF16),
            pltpu.VMEM((stages, cells, channels), BF16),
            pltpu.VMEM((cells, channels), F32),
            wide,
            wide,
            edged,
            wide,
            pltpu.VMEM((directions, cells, channels), BF16),
            pltpu.VMEM((cells, channels), F32),
            edged,
            pltpu.VMEM(((taps + 1) * 8, channels), F32),
            pltpu.VMEM((directions, channels, channels), BF16),
            pltpu.VMEM((directions, ranks, piece, channels), BF16),
            pltpu.VMEM((directions, copies, piece, channels), BF16),
            pltpu.VMEM((directions, channels, channels), BF16),
            pltpu.VMEM((directions, ranks, taps + 1, channels), F32),
            pltpu.VMEM((directions, copies, taps + 1, channels), F32),
            dma((stages, ranks)),
            dma((stages, ranks)),
            dma((directions, ranks)),
            dma((directions, ranks)),
            dma((directions, copies)),
            dma((directions, copies)),
            dma((directions, ranks)),
            dma((directions, ranks)),
            dma((directions, ranks)),
            dma((directions, ranks)),
            dma((directions, copies)),
            dma((directions, copies)),
            dma((stages,)),
            dma((5,)),
        ],
        compiler_params=pltpu.CompilerParams(
            collective_id=0, has_side_effects=True, vmem_limit_bytes=60 * 1024 * 1024
        ),
        name="mesh_block",
    )(fields, cotangent, norm_gain, kernel, mix_weight, line_order, line_starts)
    return pl.pallas_call(
        write_out,
        out_shape=outs,
        in_specs=[anywhere] * 5,
        out_specs=(hbm,) * 5,
        scratch_shapes=[dma((5,))],
        compiler_params=pltpu.CompilerParams(vmem_limit_bytes=60 * 1024 * 1024),
        name="write_out",
    )(*results)


def solution(mesh):
    in_specs = (
        P("dp", "line", None),
        P("dp", "line", None),
        P(),
        P(),
        P(),
        P(None, "line"),
        P(None, "line"),
    )
    out_specs = (P("dp", "line", None), P("dp", "line", None), P(), P(), P())
    return jax.shard_map(body, mesh=mesh, in_specs=in_specs, out_specs=out_specs, check_vma=False)
```

```python
import functools

import jax
import jax.numpy as jnp
from jax import lax
from jax.experimental import pallas as pl
from jax.experimental.pallas import tpu as pltpu
from jax.sharding import PartitionSpec as P

EPSILON = 1e-06
EDGE = 8
F32 = jnp.float32
BF16 = jnp.bfloat16


def tap_offsets(taps):
    offsets = [0]
    for dilation_level in range((taps - 1) // 2):
        offsets = offsets + [-(2**dilation_level), 2**dilation_level]
    return offsets


def fold(values):
    return jnp.sum(values.reshape(-1, 8, values.shape[1]), axis=0)


def kernel_body(
    shape,
    fields,
    cotangent,
    gain_hbm,
    taps_hbm,
    mix_hbm,
    order_hbm,
    starts_hbm,
    imitated,
    field_grad,
    mix_out,
    taps_out,
    gain_out,
    gain_ref,
    taps_ref,
    mix_ref,
    order_ref,
    starts_ref,
    gather,
    scatter,
    recv,
    placed,
    stream,
    scaled,
    inverse,
    masked,
    slope,
    activated,
    grads,
    padded,
    sums,
    parts,
    a_recv,
    b_recv,
    full,
    line_tails,
    dp_tails,
    ex_send,
    ex_recv,
    a_send,
    a_arrive,
    b_send,
    b_arrive,
    c_send,
    c_arrive,
    t_send,
    t_arrive,
    u_send,
    u_arrive,
    local_sem,
    load_sem,
):
    ranks, copies, line_len, scale = shape
    cells, channels = stream.shape
    lines = cells // line_len
    block = cells // ranks
    taps = taps_ref.shape[1]
    offsets = tap_offsets(taps)
    piece = parts.shape[1] // ranks
    me = lax.axis_index("line")
    my_dp = lax.axis_index("dp")

    loads = []
    for index, (source, target) in enumerate(
        (
            (order_hbm, order_ref),
            (gain_hbm, gain_ref),
            (taps_hbm, taps_ref),
            (starts_hbm, starts_ref),
            (mix_hbm, mix_ref),
        )
    ):
        load = pltpu.make_async_copy(source, target, load_sem.at[index])
        load.start()
        loads.append(load)

    def peer(step):
        return lax.rem(me + step, ranks)

    def dp_peer(step):
        return lax.rem(my_dp + step, copies)

    def rows(index, size):
        return pl.ds(pl.multiple_of(index * size, size), size)

    barrier = pltpu.get_barrier_semaphore()
    for step in range(1, ranks):
        pl.semaphore_signal(
            barrier, inc=1, device_id={"line": peer(step)}, device_id_type=pl.DeviceIdType.MESH
        )
    for step in range(1, copies):
        pl.semaphore_signal(
            barrier, inc=1, device_id={"dp": dp_peer(step)}, device_id_type=pl.DeviceIdType.MESH
        )
    pl.semaphore_wait(barrier, ranks - 1 + copies - 1)

    unsent = []

    def remote(source, target, send_sem, recv_sem, where):
        copy = pltpu.make_async_remote_copy(
            src_ref=source,
            dst_ref=target,
            send_sem=send_sem,
            recv_sem=recv_sem,
            device_id=where,
            device_id_type=pl.DeviceIdType.MESH,
        )
        copy.start()
        unsent.append(copy)
        return copy

    def send(stage, step, source, target):
        return remote(
            source, target, ex_send.at[stage, step], ex_recv.at[stage, step], {"line": peer(step)}
        )

    def enter(stage, array, shift):
        out = []
        for step in range(1, ranks):
            chunk = lax.rem(peer(step) + ranks * shift - shift * me, ranks)
            out.append(
                send(stage, step, array.at[0, rows(chunk, block)], recv.at[stage, rows(me, block)])
            )
        chunk = lax.rem(me + ranks * shift - shift * me, ranks)
        own = pltpu.make_async_copy(
            array.at[0, rows(chunk, block)], recv.at[stage, rows(me, block)], local_sem.at[stage]
        )
        own.start()
        return out, own

    arriving, own_fields = enter(0, fields, 0)

    def tables(direction):
        row = order_ref[direction : direction + 1, :]
        lanes = 128
        across = lax.broadcasted_iota(jnp.int32, (cells, cells), 0)
        scatter[direction] = jnp.where(across == row, 1.0, 0.0).astype(BF16)
        turned = jnp.transpose(jnp.broadcast_to(row, (lanes, cells)))
        for first in range(0, cells, lanes):
            width = lax.broadcasted_iota(jnp.int32, (cells, lanes), 1) + first
            gather[direction, :, first : first + lanes] = jnp.where(
                turned == width, 1.0, 0.0
            ).astype(BF16)

    masked[...] = jnp.zeros_like(masked)
    padded[...] = jnp.zeros_like(padded)
    for load in loads:
        load.wait()
    tables(0)

    def hand_over(stage, direction, values, sign):
        out = []
        for anchor in sorted(range(1, ranks), key=lambda step: abs(2 * step - ranks)) + [0]:
            span = pl.ds(anchor * block, block)
            chunk = jnp.dot(
                scatter[direction, span, :], values, preferred_element_type=F32
            ).astype(BF16)
            if anchor:
                placed[stage, span, :] = chunk
                step = (sign * anchor) % ranks
                out.append(send(stage, step, placed.at[stage, span], recv.at[stage, span]))
            else:
                recv[stage, span, :] = chunk
        return out

    def leave(stage, direction, values, target):
        chunk = jnp.dot(scatter[direction], values, preferred_element_type=F32)
        placed[stage] = chunk.astype(BF16)
        out = []
        for step in range(1, ranks):
            anchor = peer(step)
            where = lax.rem(me + direction * (ranks - anchor), ranks)
            out.append(
                send(
                    stage,
                    step,
                    placed.at[stage, rows(anchor, block)],
                    target.at[0, rows(where, block)],
                )
            )
        where = lax.rem(me + direction * (ranks - me), ranks)
        own = pltpu.make_async_copy(
            placed.at[stage, rows(me, block)],
            target.at[0, rows(where, block)],
            local_sem.at[stage],
        )
        own.start()
        return out, own

    def take(stage, direction, copies_in):
        for copy in copies_in:
            copy.wait_recv()
        return jnp.dot(gather[direction], recv[stage], preferred_element_type=F32)

    def keep_rows(direction, line):
        position = lax.broadcasted_iota(jnp.int32, (line_len, channels), 0)
        return position >= starts_ref[direction : direction + 1, line : line + 1]

    inside = pl.ds(EDGE, line_len)

    def forward(direction):
        for line in range(lines):
            here = pl.ds(line * line_len, line_len)
            values = stream[here, :]
            norm = lax.rsqrt(jnp.mean(values * values, axis=-1, keepdims=True) + EPSILON)
            ratio = values * norm
            normed = (ratio * gain_ref[direction : direction + 1, :]).astype(BF16).astype(F32)
            masked[direction, line, inside, :] = jnp.where(keep_rows(direction, line), normed, 0.0)
            inverse[direction, here, :] = jnp.broadcast_to(norm, (line_len, channels))
            scaled[direction, here, :] = ratio

        def one_line(line, carry):
            here = rows(line, line_len)
            inputs = masked[direction, line, inside, :]
            hidden = taps_ref[direction, 0:1, :] * inputs
            for tap in range(1, taps):
                offset = offsets[tap]
                weight = taps_ref[direction, tap : tap + 1, :]
                size = abs(offset)
                if size < EDGE:
                    near = masked[direction, line, pl.ds(EDGE + offset, line_len), :]
                    hidden = hidden + weight * near
                elif offset > 0:
                    inner = hidden[: line_len - size] + weight * inputs[size:]
                    hidden = jnp.concatenate([inner, hidden[line_len - size :]], axis=0)
                else:
                    inner = hidden[size:] + weight * inputs[: line_len - size]
                    hidden = jnp.concatenate([hidden[:size], inner], axis=0)
            gate = 0.5 * jnp.tanh(0.5 * hidden) + 0.5
            activated[direction, here, :] = (hidden * gate).astype(BF16)
            slope[direction, here, :] = gate * (1.0 + hidden * (1.0 - gate))
            return carry

        lax.fori_loop(0, lines, one_line, 0)
        mixed = jnp.dot(activated[direction], mix_ref[direction], preferred_element_type=F32)
        return (stream[...] + mixed.astype(BF16).astype(F32)).astype(BF16)

    own_fields.wait()
    stream[...] = take(0, 0, arriving)
    cot_arriving, own_cot = enter(1, cotangent, 2)
    moved = forward(0)
    arriving = hand_over(2, 0, moved, 1)
    tables(1)
    stream[...] = take(2, 1, arriving)
    moved = forward(1)
    arriving = hand_over(3, 1, moved, 1)
    tables(2)
    stream[...] = take(3, 2, arriving)
    moved = forward(2)
    out_arriving, own_out = leave(4, 2, moved, imitated)
    own_cot.wait()
    grads[...] = take(1, 2, cot_arriving)

    def backward(direction, between=None):
        back = lax.dot_general(
            grads[...].astype(BF16),
            mix_ref[direction],
            (((1,), (1,)), ((), ())),
            preferred_element_type=F32,
        )
        for line in range(lines):
            here = pl.ds(line * line_len, line_len)
            local = back[line * line_len : (line + 1) * line_len] * slope[direction, here, :]
            padded[direction, line, inside, :] = local.astype(BF16).astype(F32)

        def one_line(line, carry):
            grad = padded[direction, line, inside, :]
            total = taps_ref[direction, 0:1, :] * grad
            for tap in range(1, taps):
                offset = -offsets[tap]
                weight = taps_ref[direction, tap : tap + 1, :]
                size = abs(offset)
                if size < EDGE:
                    near = padded[direction, line, pl.ds(EDGE + offset, line_len), :]
                    total = total + weight * near
                elif offset > 0:
                    inner = total[: line_len - size] + weight * grad[size:]
                    total = jnp.concatenate([inner, total[line_len - size :]], axis=0)
                else:
                    inner = total[size:] + weight * grad[: line_len - size]
                    total = jnp.concatenate([total[:size], inner], axis=0)
            stream[rows(line, line_len), :] = total
            return carry

        lax.fori_loop(0, lines, one_line, 0)
        started = between() if between else None
        out = []
        gains = jnp.zeros((8, channels), F32)
        for line in range(lines):
            here = pl.ds(line * line_len, line_len)
            total = jnp.where(keep_rows(direction, line), stream[here, :], 0.0)
            cell = total.astype(BF16).astype(F32)
            ratio = scaled[direction, here, :]
            gains = gains + fold(cell * ratio)
            weighted = cell * gain_ref[direction : direction + 1, :]
            centre = jnp.mean(weighted * ratio, axis=-1, keepdims=True)
            change = inverse[direction, here, :] * (weighted - ratio * centre)
            out.append((grads[here, :] + change).astype(BF16))
        sums[8 * taps : 8 * taps + 8, :] = gains
        return jnp.concatenate(out, axis=0), started

    def tap_sums(direction):
        sums[0 : 8 * taps, :] = jnp.zeros((8 * taps, channels), F32)

        def one_line(line, carry):
            grad = padded[direction, line, inside, :]
            inputs = masked[direction, line, inside, :]
            for tap in range(taps):
                offset = -offsets[tap]
                size = abs(offset)
                slot = pl.ds(8 * tap, 8)
                if size == 0:
                    term = grad * inputs
                elif size < EDGE:
                    term = padded[direction, line, pl.ds(EDGE + offset, line_len), :] * inputs
                elif offset > 0:
                    term = grad[size:] * inputs[: line_len - size]
                else:
                    term = grad[: line_len - size] * inputs[size:]
                sums[slot, :] += fold(term)
            return carry

        lax.fori_loop(0, lines, one_line, 0)

    def mix_line(direction, grad_mixed):
        parts[direction] = lax.dot_general(
            activated[direction], grad_mixed, (((0,), (0,)), ((), ())), preferred_element_type=F32
        ).astype(BF16)
        return [
            remote(
                parts.at[direction, rows(peer(step), piece)],
                a_recv.at[direction, step],
                a_send.at[direction, step],
                a_arrive.at[direction, step],
                {"line": peer(step)},
            )
            for step in range(1, ranks)
        ]

    def mix_dp(direction, copies_in):
        total = parts[direction, rows(me, piece), :].astype(F32)
        for step in range(1, ranks):
            copies_in[step - 1].wait_recv()
            total = total + a_recv[direction, step].astype(F32)
        b_recv[direction, my_dp] = total.astype(BF16)
        return [
            remote(
                b_recv.at[direction, my_dp],
                b_recv.at[direction, my_dp],
                b_send.at[direction, step],
                b_arrive.at[direction, step],
                {"dp": dp_peer(step)},
            )
            for step in range(1, copies)
        ]

    def mix_spread(direction, copies_in):
        for copy in copies_in:
            copy.wait_recv()
        total = b_recv[direction, 0].astype(F32)
        for index in range(1, copies):
            total = total + b_recv[direction, index].astype(F32)
        full[direction, rows(me, piece), :] = (total * scale).astype(BF16)
        return [
            remote(
                full.at[direction, rows(me, piece)],
                full.at[direction, rows(me, piece)],
                c_send.at[direction, step],
                c_arrive.at[direction, step],
                {"line": peer(step)},
            )
            for step in range(1, ranks)
        ]

    def mix_finish(direction, copies_in):
        for copy in copies_in:
            copy.wait_recv()
        mix_out[direction] = full[direction].astype(F32)

    def tail_line(direction):
        line_tails[direction, me] = jnp.sum(sums[...].reshape(taps + 1, 8, channels), axis=1)
        return [
            remote(
                line_tails.at[direction, me],
                line_tails.at[direction, me],
                t_send.at[direction, step],
                t_arrive.at[direction, step],
                {"line": peer(step)},
            )
            for step in range(1, ranks)
        ]

    def tail_dp(direction, copies_in):
        for copy in copies_in:
            copy.wait_recv()
        total = line_tails[direction, 0]
        for index in range(1, ranks):
            total = total + line_tails[direction, index]
        dp_tails[direction, my_dp] = total
        return [
            remote(
                dp_tails.at[direction, my_dp],
                dp_tails.at[direction, my_dp],
                u_send.at[direction, step],
                u_arrive.at[direction, step],
                {"dp": dp_peer(step)},
            )
            for step in range(1, copies)
        ]

    def tail_finish(direction, copies_in):
        for copy in copies_in:
            copy.wait_recv()
        total = dp_tails[direction, 0]
        for index in range(1, copies):
            total = total + dp_tails[direction, index]
        total = total * scale
        taps_out[direction] = total[:taps]
        gain_out[direction : direction + 1, :] = total[taps : taps + 1]

    moved, _ = backward(2)
    arriving = hand_over(5, 2, moved, -1)
    a2 = mix_line(2, grads[...].astype(BF16))
    tap_sums(2)
    t2 = tail_line(2)
    grads[...] = take(5, 1, arriving)
    moved, _ = backward(1)
    arriving = hand_over(6, 1, moved, -1)
    b2 = mix_dp(2, a2)
    a1 = mix_line(1, grads[...].astype(BF16))
    tap_sums(1)
    t1 = tail_line(1)
    u2 = tail_dp(2, t2)
    grads[...] = take(6, 0, arriving)
    a0 = mix_line(0, grads[...].astype(BF16))
    b1 = mix_dp(1, a1)
    moved, b0 = backward(0, lambda: mix_dp(0, a0))
    last_arriving, own_last = leave(7, 0, moved, field_grad)
    tap_sums(0)
    t0 = tail_line(0)
    u1 = tail_dp(1, t1)
    c2 = mix_spread(2, b2)
    c1 = mix_spread(1, b1)
    c0 = mix_spread(0, b0)
    u0 = tail_dp(0, t0)
    tail_finish(2, u2)
    mix_finish(2, c2)
    mix_finish(1, c1)
    tail_finish(1, u1)
    mix_finish(0, c0)
    tail_finish(0, u0)
    for copy in out_arriving + last_arriving:
        copy.wait_recv()
    own_out.wait()
    own_last.wait()
    for copy in unsent:
        copy.wait_send()


def write_out(*refs):
    count = (len(refs) - 2) // 3
    sources, targets, held = refs[:count], refs[count : 2 * count], refs[2 * count : 3 * count]
    in_sem, out_sem = refs[-2:]
    into = [
        pltpu.make_async_copy(sources[index], held[index], in_sem.at[index])
        for index in range(count)
    ]
    out = [
        pltpu.make_async_copy(held[index], targets[index], out_sem.at[index])
        for index in range(count)
    ]
    for move in into:
        move.start()
    for index in range(count):
        into[index].wait()
        out[index].start()
    for move in out:
        move.wait()


def body(fields, cotangent, norm_gain, kernel, mix_weight, line_order, line_starts):
    ranks = lax.axis_size("line")
    copies = lax.axis_size("dp")
    batch, cells, channels = fields.shape
    assert batch == 1
    directions, taps = kernel.shape[:2]
    lines = line_starts.shape[1]
    line_len = cells // lines
    scale = float(copies * batch * ranks * cells) ** (-0.5)
    piece = channels // ranks
    stages = 2 * directions + 2
    vmem = pl.BlockSpec(memory_space=pltpu.VMEM)
    hbm = pl.BlockSpec(memory_space=pltpu.HBM)
    anywhere = pl.BlockSpec(memory_space=pl.ANY)
    wide = pltpu.VMEM((directions, cells, channels), F32)
    edged = pltpu.VMEM((directions, lines, line_len + 2 * EDGE, channels), F32)
    dma = pltpu.SemaphoreType.DMA
    outs = (
        jax.ShapeDtypeStruct(fields.shape, BF16),
        jax.ShapeDtypeStruct(fields.shape, BF16),
        jax.ShapeDtypeStruct((directions, channels, channels), F32),
        jax.ShapeDtypeStruct((directions, taps, channels), F32),
        jax.ShapeDtypeStruct((directions, channels), F32),
    )
    results = pl.pallas_call(
        functools.partial(kernel_body, (ranks, copies, line_len, scale)),
        out_shape=outs,
        in_specs=[hbm] * 7,
        out_specs=(anywhere, anywhere, vmem, vmem, vmem),
        scratch_shapes=[
            pltpu.VMEM(norm_gain.shape, F32),
            pltpu.VMEM(kernel.shape, F32),
            pltpu.VMEM(mix_weight.shape, BF16),
            pltpu.VMEM(line_order.shape, jnp.int32),
            pltpu.VMEM(line_starts.shape, jnp.int32),
            pltpu.VMEM((directions, cells, cells), BF16),
            pltpu.VMEM((directions, cells, cells), BF16),
            pltpu.VMEM((stages, cells, channels), BF16),
            pltpu.VMEM((stages, cells, channels), BF16),
            pltpu.VMEM((cells, channels), F32),
            wide,
            wide,
            edged,
            wide,
            pltpu.VMEM((directions, cells, channels), BF16),
            pltpu.VMEM((cells, channels), F32),
            edged,
            pltpu.VMEM(((taps + 1) * 8, channels), F32),
            pltpu.VMEM((directions, channels, channels), BF16),
            pltpu.VMEM((directions, ranks, piece, channels), BF16),
            pltpu.VMEM((directions, copies, piece, channels), BF16),
            pltpu.VMEM((directions, channels, channels), BF16),
            pltpu.VMEM((directions, ranks, taps + 1, channels), F32),
            pltpu.VMEM((directions, copies, taps + 1, channels), F32),
            dma((stages, ranks)),
            dma((stages, ranks)),
            dma((directions, ranks)),
            dma((directions, ranks)),
            dma((directions, copies)),
            dma((directions, copies)),
            dma((directions, ranks)),
            dma((directions, ranks)),
            dma((directions, ranks)),
            dma((directions, ranks)),
            dma((directions, copies)),
            dma((directions, copies)),
            dma((stages,)),
            dma((5,)),
        ],
        compiler_params=pltpu.CompilerParams(
            collective_id=0, has_side_effects=True, vmem_limit_bytes=60 * 1024 * 1024
        ),
        name="mesh_block",
    )(fields, cotangent, norm_gain, kernel, mix_weight, line_order, line_starts)
    return pl.pallas_call(
        write_out,
        out_shape=outs,
        in_specs=[anywhere] * 5,
        out_specs=(hbm,) * 5,
        scratch_shapes=[pltpu.VMEM(out.shape, out.dtype) for out in outs] + [dma((5,)), dma((5,))],
        compiler_params=pltpu.CompilerParams(vmem_limit_bytes=60 * 1024 * 1024),
        name="write_out",
    )(*results)


def solution(mesh):
    in_specs = (
        P("dp", "line", None),
        P("dp", "line", None),
        P(),
        P(),
        P(),
        P(None, "line"),
        P(None, "line"),
    )
    out_specs = (P("dp", "line", None), P("dp", "line", None), P(), P(), P())
    return jax.shard_map(body, mesh=mesh, in_specs=in_specs, out_specs=out_specs, check_vma=False)
```

```python
import functools

import jax
import jax.numpy as jnp
from jax import lax
from jax.experimental import pallas as pl
from jax.experimental.pallas import tpu as pltpu
from jax.sharding import PartitionSpec as P

EPSILON = 1e-06
EDGE = 8
F32 = jnp.float32
BF16 = jnp.bfloat16


def tap_offsets(taps):
    offsets = [0]
    for dilation_level in range((taps - 1) // 2):
        offsets = offsets + [-(2**dilation_level), 2**dilation_level]
    return offsets


def fold(values):
    return jnp.sum(values.reshape(-1, 8, values.shape[1]), axis=0)


def kernel_body(
    shape,
    fields,
    cotangent,
    gain_hbm,
    taps_hbm,
    mix_hbm,
    order_hbm,
    starts_hbm,
    imitated,
    field_grad,
    mix_out,
    taps_out,
    gain_out,
    gain_ref,
    taps_ref,
    mix_ref,
    order_ref,
    starts_ref,
    gather,
    scatter,
    recv,
    placed,
    stream,
    scaled,
    inverse,
    masked,
    slope,
    activated,
    grads,
    padded,
    sums,
    parts,
    a_recv,
    b_recv,
    full,
    line_tails,
    dp_tails,
    ex_send,
    ex_recv,
    a_send,
    a_arrive,
    b_send,
    b_arrive,
    c_send,
    c_arrive,
    t_send,
    t_arrive,
    u_send,
    u_arrive,
    local_sem,
    load_sem,
):
    ranks, copies, line_len, scale = shape
    cells, channels = stream.shape
    lines = cells // line_len
    block = cells // ranks
    taps = taps_ref.shape[1]
    offsets = tap_offsets(taps)
    piece = channels // ranks
    me = lax.axis_index("line")
    my_dp = lax.axis_index("dp")

    loads = []
    for index, (source, target) in enumerate(
        (
            (order_hbm, order_ref),
            (gain_hbm, gain_ref),
            (taps_hbm, taps_ref),
            (starts_hbm, starts_ref),
            (mix_hbm, mix_ref),
        )
    ):
        load = pltpu.make_async_copy(source, target, load_sem.at[index])
        load.start()
        loads.append(load)

    def peer(step):
        return lax.rem(me + step, ranks)

    def dp_peer(step):
        return lax.rem(my_dp + step, copies)

    def rows(index, size):
        return pl.ds(pl.multiple_of(index * size, size), size)

    barrier = pltpu.get_barrier_semaphore()
    for step in range(1, ranks):
        pl.semaphore_signal(
            barrier, inc=1, device_id={"line": peer(step)}, device_id_type=pl.DeviceIdType.MESH
        )
    for step in range(1, copies):
        pl.semaphore_signal(
            barrier, inc=1, device_id={"dp": dp_peer(step)}, device_id_type=pl.DeviceIdType.MESH
        )
    pl.semaphore_wait(barrier, ranks - 1 + copies - 1)

    unsent = []

    def remote(source, target, send_sem, recv_sem, where):
        copy = pltpu.make_async_remote_copy(
            src_ref=source,
            dst_ref=target,
            send_sem=send_sem,
            recv_sem=recv_sem,
            device_id=where,
            device_id_type=pl.DeviceIdType.MESH,
        )
        copy.start()
        unsent.append(copy)
        return copy

    def send(stage, step, source, target):
        return remote(
            source, target, ex_send.at[stage, step], ex_recv.at[stage, step], {"line": peer(step)}
        )

    def enter(stage, array, shift):
        out = []
        for step in range(1, ranks):
            chunk = lax.rem(peer(step) + ranks * shift - shift * me, ranks)
            out.append(
                send(stage, step, array.at[0, rows(chunk, block)], recv.at[stage, rows(me, block)])
            )
        chunk = lax.rem(me + ranks * shift - shift * me, ranks)
        own = pltpu.make_async_copy(
            array.at[0, rows(chunk, block)], recv.at[stage, rows(me, block)], local_sem.at[stage]
        )
        own.start()
        return out, own

    arriving, own_fields = enter(0, fields, 0)

    def tables(direction):
        lanes = 128

        def one_part(part, carry):
            span = rows(part, lanes)
            across = lax.broadcasted_iota(jnp.int32, (lanes, cells), 0) + part * lanes
            row = order_ref[direction : direction + 1, :]
            scatter[direction, span, :] = jnp.where(across == row, 1.0, 0.0).astype(BF16)
            some = order_ref[direction : direction + 1, span]
            turned = jnp.transpose(jnp.broadcast_to(some, (lanes, lanes)))
            for first in range(0, cells, lanes):
                width = lax.broadcasted_iota(jnp.int32, (lanes, lanes), 1) + first
                gather[direction, span, first : first + lanes] = jnp.where(
                    turned == width, 1.0, 0.0
                ).astype(BF16)
            return carry

        lax.fori_loop(0, cells // lanes, one_part, 0)

    masked[...] = jnp.zeros_like(masked)
    padded[...] = jnp.zeros_like(padded)
    for load in loads:
        load.wait()
    tables(0)

    def hand_over(stage, direction, values, sign):
        out = []
        for anchor in sorted(range(1, ranks), key=lambda step: abs(2 * step - ranks)) + [0]:
            span = pl.ds(anchor * block, block)
            chunk = jnp.dot(
                scatter[direction, span, :], values, preferred_element_type=F32
            ).astype(BF16)
            if anchor:
                placed[stage, span, :] = chunk
                step = (sign * anchor) % ranks
                out.append(send(stage, step, placed.at[stage, span], recv.at[stage, span]))
            else:
                recv[stage, span, :] = chunk
        return out

    def leave(stage, direction, values, target):
        chunk = jnp.dot(scatter[direction], values, preferred_element_type=F32)
        placed[stage] = chunk.astype(BF16)
        out = []
        for step in range(1, ranks):
            anchor = peer(step)
            where = lax.rem(me + direction * (ranks - anchor), ranks)
            out.append(
                send(
                    stage,
                    step,
                    placed.at[stage, rows(anchor, block)],
                    target.at[0, rows(where, block)],
                )
            )
        where = lax.rem(me + direction * (ranks - me), ranks)
        own = pltpu.make_async_copy(
            placed.at[stage, rows(me, block)],
            target.at[0, rows(where, block)],
            local_sem.at[stage],
        )
        own.start()
        return out, own

    def take(stage, direction, copies_in):
        for copy in copies_in:
            copy.wait_recv()
        return jnp.dot(gather[direction], recv[stage], preferred_element_type=F32)

    def keep_rows(direction, line):
        position = lax.broadcasted_iota(jnp.int32, (line_len, channels), 0)
        return position >= starts_ref[direction : direction + 1, line : line + 1]

    inside = pl.ds(EDGE, line_len)

    def forward(direction):
        for line in range(lines):
            here = pl.ds(line * line_len, line_len)
            values = stream[here, :]
            norm = lax.rsqrt(jnp.mean(values * values, axis=-1, keepdims=True) + EPSILON)
            ratio = values * norm
            normed = (ratio * gain_ref[direction : direction + 1, :]).astype(BF16).astype(F32)
            masked[direction, line, inside, :] = jnp.where(keep_rows(direction, line), normed, 0.0)
            inverse[direction, here, :] = jnp.broadcast_to(norm, (line_len, channels))
            scaled[direction, here, :] = ratio

        def one_line(line, carry):
            here = rows(line, line_len)
            inputs = masked[direction, line, inside, :]
            hidden = taps_ref[direction, 0:1, :] * inputs
            for tap in range(1, taps):
                offset = offsets[tap]
                weight = taps_ref[direction, tap : tap + 1, :]
                size = abs(offset)
                if size < EDGE:
                    near = masked[direction, line, pl.ds(EDGE + offset, line_len), :]
                    hidden = hidden + weight * near
                elif offset > 0:
                    inner = hidden[: line_len - size] + weight * inputs[size:]
                    hidden = jnp.concatenate([inner, hidden[line_len - size :]], axis=0)
                else:
                    inner = hidden[size:] + weight * inputs[: line_len - size]
                    hidden = jnp.concatenate([hidden[:size], inner], axis=0)
            gate = 0.5 * jnp.tanh(0.5 * hidden) + 0.5
            activated[direction, here, :] = (hidden * gate).astype(BF16)
            slope[direction, here, :] = gate * (1.0 + hidden * (1.0 - gate))
            return carry

        lax.fori_loop(0, lines, one_line, 0)
        mixed = jnp.dot(activated[direction], mix_ref[direction], preferred_element_type=F32)
        return (stream[...] + mixed.astype(BF16).astype(F32)).astype(BF16)

    own_fields.wait()
    stream[...] = take(0, 0, arriving)
    cot_arriving, own_cot = enter(1, cotangent, 2)
    moved = forward(0)
    arriving = hand_over(2, 0, moved, 1)
    tables(1)
    stream[...] = take(2, 1, arriving)
    moved = forward(1)
    arriving = hand_over(3, 1, moved, 1)
    tables(2)
    stream[...] = take(3, 2, arriving)
    moved = forward(2)
    out_arriving, own_out = leave(4, 2, moved, imitated)
    own_cot.wait()
    grads[...] = take(1, 2, cot_arriving)

    def backward(direction, between=None):
        back = lax.dot_general(
            grads[...].astype(BF16),
            mix_ref[direction],
            (((1,), (1,)), ((), ())),
            preferred_element_type=F32,
        )
        for line in range(lines):
            here = pl.ds(line * line_len, line_len)
            local = back[line * line_len : (line + 1) * line_len] * slope[direction, here, :]
            padded[direction, line, inside, :] = local.astype(BF16).astype(F32)

        def one_line(line, carry):
            grad = padded[direction, line, inside, :]
            total = taps_ref[direction, 0:1, :] * grad
            for tap in range(1, taps):
                offset = -offsets[tap]
                weight = taps_ref[direction, tap : tap + 1, :]
                size = abs(offset)
                if size < EDGE:
                    near = padded[direction, line, pl.ds(EDGE + offset, line_len), :]
                    total = total + weight * near
                elif offset > 0:
                    inner = total[: line_len - size] + weight * grad[size:]
                    total = jnp.concatenate([inner, total[line_len - size :]], axis=0)
                else:
                    inner = total[size:] + weight * grad[: line_len - size]
                    total = jnp.concatenate([total[:size], inner], axis=0)
            stream[rows(line, line_len), :] = total
            return carry

        lax.fori_loop(0, lines, one_line, 0)
        started = between() if between else None
        out = []
        gains = jnp.zeros((8, channels), F32)
        for line in range(lines):
            here = pl.ds(line * line_len, line_len)
            total = jnp.where(keep_rows(direction, line), stream[here, :], 0.0)
            cell = total.astype(BF16).astype(F32)
            ratio = scaled[direction, here, :]
            gains = gains + fold(cell * ratio)
            weighted = cell * gain_ref[direction : direction + 1, :]
            centre = jnp.mean(weighted * ratio, axis=-1, keepdims=True)
            change = inverse[direction, here, :] * (weighted - ratio * centre)
            out.append((grads[here, :] + change).astype(BF16))
        sums[8 * taps : 8 * taps + 8, :] = gains
        return jnp.concatenate(out, axis=0), started

    def tap_sums(direction):
        sums[0 : 8 * taps, :] = jnp.zeros((8 * taps, channels), F32)

        def one_line(line, carry):
            grad = padded[direction, line, inside, :]
            inputs = masked[direction, line, inside, :]
            for tap in range(taps):
                offset = -offsets[tap]
                size = abs(offset)
                slot = pl.ds(8 * tap, 8)
                if size == 0:
                    term = grad * inputs
                elif size < EDGE:
                    term = padded[direction, line, pl.ds(EDGE + offset, line_len), :] * inputs
                elif offset > 0:
                    term = grad[size:] * inputs[: line_len - size]
                else:
                    term = grad[: line_len - size] * inputs[size:]
                sums[slot, :] += fold(term)
            return carry

        lax.fori_loop(0, lines, one_line, 0)

    directions = parts.shape[1]
    spans = (pl.ds(0, 1), pl.ds(1, directions - 1))

    def mix_part(direction, grad_mixed):
        part = lax.dot_general(
            activated[direction], grad_mixed, (((0,), (0,)), ((), ())), preferred_element_type=F32
        ).astype(BF16)
        for rank in range(ranks):
            parts[rank, direction] = part[rank * piece : (rank + 1) * piece]

    def mix_line(group):
        return [
            remote(
                parts.at[peer(step), spans[group]],
                a_recv.at[step, spans[group]],
                a_send.at[group, step],
                a_arrive.at[group, step],
                {"line": peer(step)},
            )
            for step in range(1, ranks)
        ]

    def mix_dp(group, copies_in):
        span = spans[group]
        total = parts[me, span].astype(F32)
        for step in range(1, ranks):
            copies_in[step - 1].wait_recv()
            total = total + a_recv[step, span].astype(F32)
        b_recv[my_dp, span] = total.astype(BF16)
        return [
            remote(
                b_recv.at[my_dp, span],
                b_recv.at[my_dp, span],
                b_send.at[group, step],
                b_arrive.at[group, step],
                {"dp": dp_peer(step)},
            )
            for step in range(1, copies)
        ]

    def mix_spread(group, copies_in):
        span = spans[group]
        for copy in copies_in:
            copy.wait_recv()
        total = b_recv[0, span].astype(F32)
        for index in range(1, copies):
            total = total + b_recv[index, span].astype(F32)
        full[me, span] = (total * scale).astype(BF16)
        return [
            remote(
                full.at[me, span],
                full.at[me, span],
                c_send.at[group, step],
                c_arrive.at[group, step],
                {"line": peer(step)},
            )
            for step in range(1, ranks)
        ]

    def mix_finish(group, copies_in):
        for copy in copies_in:
            copy.wait_recv()
        for direction in range(group, directions if group else 1):
            for rank in range(ranks):
                mix_out[direction, rank * piece : (rank + 1) * piece, :] = full[
                    rank, direction
                ].astype(F32)

    def tail_part(direction):
        line_tails[me, direction] = jnp.sum(sums[...].reshape(taps + 1, 8, channels), axis=1)

    def tail_line(group):
        span = spans[group]
        return [
            remote(
                line_tails.at[me, span],
                line_tails.at[me, span],
                t_send.at[group, step],
                t_arrive.at[group, step],
                {"line": peer(step)},
            )
            for step in range(1, ranks)
        ]

    def tail_dp(group, copies_in):
        span = spans[group]
        for copy in copies_in:
            copy.wait_recv()
        total = line_tails[0, span]
        for index in range(1, ranks):
            total = total + line_tails[index, span]
        dp_tails[my_dp, span] = total
        return [
            remote(
                dp_tails.at[my_dp, span],
                dp_tails.at[my_dp, span],
                u_send.at[group, step],
                u_arrive.at[group, step],
                {"dp": dp_peer(step)},
            )
            for step in range(1, copies)
        ]

    def tail_finish(group, copies_in):
        for copy in copies_in:
            copy.wait_recv()
        for direction in range(group, directions if group else 1):
            total = dp_tails[0, direction]
            for index in range(1, copies):
                total = total + dp_tails[index, direction]
            total = total * scale
            taps_out[direction] = total[:taps]
            gain_out[direction : direction + 1, :] = total[taps : taps + 1]

    moved, _ = backward(2)
    arriving = hand_over(5, 2, moved, -1)
    mix_part(2, grads[...].astype(BF16))
    tap_sums(2)
    tail_part(2)
    grads[...] = take(5, 1, arriving)
    moved, _ = backward(1)
    arriving = hand_over(6, 1, moved, -1)
    mix_part(1, grads[...].astype(BF16))
    a1 = mix_line(1)
    tap_sums(1)
    tail_part(1)
    t1 = tail_line(1)
    b1 = mix_dp(1, a1)
    grads[...] = take(6, 0, arriving)
    mix_part(0, grads[...].astype(BF16))
    a0 = mix_line(0)
    u1 = tail_dp(1, t1)
    moved, b0 = backward(0, lambda: mix_dp(0, a0))
    last_arriving, own_last = leave(7, 0, moved, field_grad)
    tap_sums(0)
    tail_part(0)
    t0 = tail_line(0)
    c1 = mix_spread(1, b1)
    c0 = mix_spread(0, b0)
    u0 = tail_dp(0, t0)
    tail_finish(1, u1)
    mix_finish(1, c1)
    mix_finish(0, c0)
    tail_finish(0, u0)
    for copy in out_arriving + last_arriving:
        copy.wait_recv()
    own_out.wait()
    own_last.wait()
    for copy in unsent:
        copy.wait_send()


def write_out(*refs):
    count = (len(refs) - 2) // 3
    sources, targets, held = refs[:count], refs[count : 2 * count], refs[2 * count : 3 * count]
    in_sem, out_sem = refs[-2:]
    into = [
        pltpu.make_async_copy(sources[index], held[index], in_sem.at[index])
        for index in range(count)
    ]
    out = [
        pltpu.make_async_copy(held[index], targets[index], out_sem.at[index])
        for index in range(count)
    ]
    for move in into:
        move.start()
    for index in range(count):
        into[index].wait()
        out[index].start()
    for move in out:
        move.wait()


def body(fields, cotangent, norm_gain, kernel, mix_weight, line_order, line_starts):
    ranks = lax.axis_size("line")
    copies = lax.axis_size("dp")
    batch, cells, channels = fields.shape
    assert batch == 1
    directions, taps = kernel.shape[:2]
    lines = line_starts.shape[1]
    line_len = cells // lines
    scale = float(copies * batch * ranks * cells) ** (-0.5)
    piece = channels // ranks
    stages = 2 * directions + 2
    vmem = pl.BlockSpec(memory_space=pltpu.VMEM)
    hbm = pl.BlockSpec(memory_space=pltpu.HBM)
    anywhere = pl.BlockSpec(memory_space=pl.ANY)
    wide = pltpu.VMEM((directions, cells, channels), F32)
    edged = pltpu.VMEM((directions, lines, line_len + 2 * EDGE, channels), F32)
    dma = pltpu.SemaphoreType.DMA
    outs = (
        jax.ShapeDtypeStruct(fields.shape, BF16),
        jax.ShapeDtypeStruct(fields.shape, BF16),
        jax.ShapeDtypeStruct((directions, channels, channels), F32),
        jax.ShapeDtypeStruct((directions, taps, channels), F32),
        jax.ShapeDtypeStruct((directions, channels), F32),
    )
    results = pl.pallas_call(
        functools.partial(kernel_body, (ranks, copies, line_len, scale)),
        out_shape=outs,
        in_specs=[hbm] * 7,
        out_specs=(anywhere, anywhere, vmem, vmem, vmem),
        scratch_shapes=[
            pltpu.VMEM(norm_gain.shape, F32),
            pltpu.VMEM(kernel.shape, F32),
            pltpu.VMEM(mix_weight.shape, BF16),
            pltpu.VMEM(line_order.shape, jnp.int32),
            pltpu.VMEM(line_starts.shape, jnp.int32),
            pltpu.VMEM((directions, cells, cells), BF16),
            pltpu.VMEM((directions, cells, cells), BF16),
            pltpu.VMEM((stages, cells, channels), BF16),
            pltpu.VMEM((stages, cells, channels), BF16),
            pltpu.VMEM((cells, channels), F32),
            wide,
            wide,
            edged,
            wide,
            pltpu.VMEM((directions, cells, channels), BF16),
            pltpu.VMEM((cells, channels), F32),
            edged,
            pltpu.VMEM(((taps + 1) * 8, channels), F32),
            pltpu.VMEM((ranks, directions, piece, channels), BF16),
            pltpu.VMEM((ranks, directions, piece, channels), BF16),
            pltpu.VMEM((copies, directions, piece, channels), BF16),
            pltpu.VMEM((ranks, directions, piece, channels), BF16),
            pltpu.VMEM((ranks, directions, taps + 1, channels), F32),
            pltpu.VMEM((copies, directions, taps + 1, channels), F32),
            dma((stages, ranks)),
            dma((stages, ranks)),
            dma((2, ranks)),
            dma((2, ranks)),
            dma((2, copies)),
            dma((2, copies)),
            dma((2, ranks)),
            dma((2, ranks)),
            dma((2, ranks)),
            dma((2, ranks)),
            dma((2, copies)),
            dma((2, copies)),
            dma((stages,)),
            dma((5,)),
        ],
        compiler_params=pltpu.CompilerParams(
            collective_id=0, has_side_effects=True, vmem_limit_bytes=60 * 1024 * 1024
        ),
        name="mesh_block",
    )(fields, cotangent, norm_gain, kernel, mix_weight, line_order, line_starts)
    return pl.pallas_call(
        write_out,
        out_shape=outs,
        in_specs=[anywhere] * 5,
        out_specs=(hbm,) * 5,
        scratch_shapes=[pltpu.VMEM(out.shape, out.dtype) for out in outs] + [dma((5,)), dma((5,))],
        compiler_params=pltpu.CompilerParams(vmem_limit_bytes=60 * 1024 * 1024),
        name="write_out",
    )(*results)


def solution(mesh):
    in_specs = (
        P("dp", "line", None),
        P("dp", "line", None),
        P(),
        P(),
        P(),
        P(None, "line"),
        P(None, "line"),
    )
    out_specs = (P("dp", "line", None), P("dp", "line", None), P(), P(), P())
    return jax.shard_map(body, mesh=mesh, in_specs=in_specs, out_specs=out_specs, check_vma=False)
```

```python
import functools

import jax
import jax.numpy as jnp
from jax import lax
from jax.experimental import pallas as pl
from jax.experimental.pallas import tpu as pltpu
from jax.sharding import PartitionSpec as P

EPSILON = 1e-06
EDGE = 8
F32 = jnp.float32
BF16 = jnp.bfloat16


def tap_offsets(taps):
    offsets = [0]
    for dilation_level in range((taps - 1) // 2):
        offsets = offsets + [-(2**dilation_level), 2**dilation_level]
    return offsets


def fold(values):
    return jnp.sum(values.reshape(-1, 8, values.shape[1]), axis=0)


def kernel_body(
    shape,
    fields,
    cotangent,
    gain_hbm,
    taps_hbm,
    mix_hbm,
    order_hbm,
    starts_hbm,
    imitated,
    field_grad,
    mix_out,
    taps_out,
    gain_out,
    gain_ref,
    taps_ref,
    mix_ref,
    order_ref,
    starts_ref,
    gather,
    scatter,
    recv,
    placed,
    stream,
    scaled,
    inverse,
    masked,
    slope,
    activated,
    grads,
    padded,
    sums,
    parts,
    a_recv,
    b_recv,
    full,
    line_tails,
    dp_tails,
    ex_send,
    ex_recv,
    a_send,
    a_arrive,
    b_send,
    b_arrive,
    c_send,
    c_arrive,
    t_send,
    t_arrive,
    u_send,
    u_arrive,
    local_sem,
    load_sem,
):
    ranks, copies, line_len, scale = shape
    cells, channels = stream.shape
    lines = cells // line_len
    block = cells // ranks
    taps = taps_ref.shape[1]
    offsets = tap_offsets(taps)
    piece = parts.shape[1] // ranks
    me = lax.axis_index("line")
    my_dp = lax.axis_index("dp")

    loads = []
    for index, (source, target) in enumerate(
        (
            (order_hbm, order_ref),
            (gain_hbm, gain_ref),
            (taps_hbm, taps_ref),
            (starts_hbm, starts_ref),
            (mix_hbm, mix_ref),
        )
    ):
        load = pltpu.make_async_copy(source, target, load_sem.at[index])
        load.start()
        loads.append(load)

    def peer(step):
        return lax.rem(me + step, ranks)

    def dp_peer(step):
        return lax.rem(my_dp + step, copies)

    def rows(index, size):
        return pl.ds(pl.multiple_of(index * size, size), size)

    barrier = pltpu.get_barrier_semaphore()
    for step in range(1, ranks):
        pl.semaphore_signal(
            barrier, inc=1, device_id={"line": peer(step)}, device_id_type=pl.DeviceIdType.MESH
        )
    for step in range(1, copies):
        pl.semaphore_signal(
            barrier, inc=1, device_id={"dp": dp_peer(step)}, device_id_type=pl.DeviceIdType.MESH
        )
    pl.semaphore_wait(barrier, ranks - 1 + copies - 1)

    unsent = []

    def remote(source, target, send_sem, recv_sem, where):
        copy = pltpu.make_async_remote_copy(
            src_ref=source,
            dst_ref=target,
            send_sem=send_sem,
            recv_sem=recv_sem,
            device_id=where,
            device_id_type=pl.DeviceIdType.MESH,
        )
        copy.start()
        unsent.append(copy)
        return copy

    def send(stage, step, source, target):
        return remote(
            source, target, ex_send.at[stage, step], ex_recv.at[stage, step], {"line": peer(step)}
        )

    def enter(stage, array, shift):
        out = []
        for step in range(1, ranks):
            chunk = lax.rem(peer(step) + ranks * shift - shift * me, ranks)
            out.append(
                send(stage, step, array.at[0, rows(chunk, block)], recv.at[stage, rows(me, block)])
            )
        chunk = lax.rem(me + ranks * shift - shift * me, ranks)
        own = pltpu.make_async_copy(
            array.at[0, rows(chunk, block)], recv.at[stage, rows(me, block)], local_sem.at[stage]
        )
        own.start()
        return out, own

    arriving, own_fields = enter(0, fields, 0)

    def tables(direction):
        row = order_ref[direction : direction + 1, :]
        lanes = 128
        across = lax.broadcasted_iota(jnp.int32, (cells, cells), 0)
        scatter[direction] = jnp.where(across == row, 1.0, 0.0).astype(BF16)
        turned = jnp.transpose(jnp.broadcast_to(row, (lanes, cells)))
        for first in range(0, cells, lanes):
            width = lax.broadcasted_iota(jnp.int32, (cells, lanes), 1) + first
            gather[direction, :, first : first + lanes] = jnp.where(
                turned == width, 1.0, 0.0
            ).astype(BF16)

    masked[...] = jnp.zeros_like(masked)
    padded[...] = jnp.zeros_like(padded)
    for load in loads:
        load.wait()
    tables(0)

    def hand_over(stage, direction, values, sign):
        out = []
        for anchor in list(range(1, ranks)) + [0]:
            span = pl.ds(anchor * block, block)
            chunk = jnp.dot(
                scatter[direction, span, :], values, preferred_element_type=F32
            ).astype(BF16)
            if anchor:
                placed[stage, span, :] = chunk
                step = (sign * anchor) % ranks
                out.append(send(stage, step, placed.at[stage, span], recv.at[stage, span]))
            else:
                recv[stage, span, :] = chunk
        return out

    def leave(stage, direction, values, target):
        chunk = jnp.dot(scatter[direction], values, preferred_element_type=F32)
        placed[stage] = chunk.astype(BF16)
        out = []
        for step in range(1, ranks):
            anchor = peer(step)
            where = lax.rem(me + direction * (ranks - anchor), ranks)
            out.append(
                send(
                    stage,
                    step,
                    placed.at[stage, rows(anchor, block)],
                    target.at[0, rows(where, block)],
                )
            )
        where = lax.rem(me + direction * (ranks - me), ranks)
        own = pltpu.make_async_copy(
            placed.at[stage, rows(me, block)],
            target.at[0, rows(where, block)],
            local_sem.at[stage],
        )
        own.start()
        return out, own

    def take(stage, direction, copies_in):
        for copy in copies_in:
            copy.wait_recv()
        return jnp.dot(gather[direction], recv[stage], preferred_element_type=F32)

    def keep_rows(direction, line):
        position = lax.broadcasted_iota(jnp.int32, (line_len, channels), 0)
        return position >= starts_ref[direction : direction + 1, line : line + 1]

    inside = pl.ds(EDGE, line_len)

    def forward(direction):
        for line in range(lines):
            here = pl.ds(line * line_len, line_len)
            values = stream[here, :]
            norm = lax.rsqrt(jnp.mean(values * values, axis=-1, keepdims=True) + EPSILON)
            ratio = values * norm
            normed = (ratio * gain_ref[direction : direction + 1, :]).astype(BF16).astype(F32)
            masked[direction, line, inside, :] = jnp.where(keep_rows(direction, line), normed, 0.0)
            inverse[direction, here, :] = jnp.broadcast_to(norm, (line_len, channels))
            scaled[direction, here, :] = ratio

        def one_line(line, carry):
            here = rows(line, line_len)
            inputs = masked[direction, line, inside, :]
            hidden = taps_ref[direction, 0:1, :] * inputs
            for tap in range(1, taps):
                offset = offsets[tap]
                weight = taps_ref[direction, tap : tap + 1, :]
                size = abs(offset)
                if size < EDGE:
                    near = masked[direction, line, pl.ds(EDGE + offset, line_len), :]
                    hidden = hidden + weight * near
                elif offset > 0:
                    inner = hidden[: line_len - size] + weight * inputs[size:]
                    hidden = jnp.concatenate([inner, hidden[line_len - size :]], axis=0)
                else:
                    inner = hidden[size:] + weight * inputs[: line_len - size]
                    hidden = jnp.concatenate([hidden[:size], inner], axis=0)
            gate = 0.5 * jnp.tanh(0.5 * hidden) + 0.5
            activated[direction, here, :] = (hidden * gate).astype(BF16)
            slope[direction, here, :] = gate * (1.0 + hidden * (1.0 - gate))
            return carry

        lax.fori_loop(0, lines, one_line, 0)
        mixed = jnp.dot(activated[direction], mix_ref[direction], preferred_element_type=F32)
        return (stream[...] + mixed.astype(BF16).astype(F32)).astype(BF16)

    own_fields.wait()
    stream[...] = take(0, 0, arriving)
    cot_arriving, own_cot = enter(1, cotangent, 2)
    moved = forward(0)
    arriving = hand_over(2, 0, moved, 1)
    tables(1)
    stream[...] = take(2, 1, arriving)
    moved = forward(1)
    arriving = hand_over(3, 1, moved, 1)
    tables(2)
    stream[...] = take(3, 2, arriving)
    moved = forward(2)
    out_arriving, own_out = leave(4, 2, moved, imitated)
    own_cot.wait()
    grads[...] = take(1, 2, cot_arriving)

    def backward(direction):
        back = lax.dot_general(
            grads[...].astype(BF16),
            mix_ref[direction],
            (((1,), (1,)), ((), ())),
            preferred_element_type=F32,
        )
        for line in range(lines):
            here = pl.ds(line * line_len, line_len)
            local = back[line * line_len : (line + 1) * line_len] * slope[direction, here, :]
            padded[direction, line, inside, :] = local.astype(BF16).astype(F32)

        def one_line(line, carry):
            grad = padded[direction, line, inside, :]
            total = taps_ref[direction, 0:1, :] * grad
            for tap in range(1, taps):
                offset = -offsets[tap]
                weight = taps_ref[direction, tap : tap + 1, :]
                size = abs(offset)
                if size < EDGE:
                    near = padded[direction, line, pl.ds(EDGE + offset, line_len), :]
                    total = total + weight * near
                elif offset > 0:
                    inner = total[: line_len - size] + weight * grad[size:]
                    total = jnp.concatenate([inner, total[line_len - size :]], axis=0)
                else:
                    inner = total[size:] + weight * grad[: line_len - size]
                    total = jnp.concatenate([total[:size], inner], axis=0)
            stream[rows(line, line_len), :] = total
            return carry

        lax.fori_loop(0, lines, one_line, 0)
        out = []
        gains = jnp.zeros((8, channels), F32)
        for line in range(lines):
            here = pl.ds(line * line_len, line_len)
            total = jnp.where(keep_rows(direction, line), stream[here, :], 0.0)
            cell = total.astype(BF16).astype(F32)
            ratio = scaled[direction, here, :]
            gains = gains + fold(cell * ratio)
            weighted = cell * gain_ref[direction : direction + 1, :]
            centre = jnp.mean(weighted * ratio, axis=-1, keepdims=True)
            change = inverse[direction, here, :] * (weighted - ratio * centre)
            out.append((grads[here, :] + change).astype(BF16))
        sums[8 * taps : 8 * taps + 8, :] = gains
        return jnp.concatenate(out, axis=0)

    def tap_sums(direction):
        sums[0 : 8 * taps, :] = jnp.zeros((8 * taps, channels), F32)

        def one_line(line, carry):
            grad = padded[direction, line, inside, :]
            inputs = masked[direction, line, inside, :]
            for tap in range(taps):
                offset = -offsets[tap]
                size = abs(offset)
                slot = pl.ds(8 * tap, 8)
                if size == 0:
                    term = grad * inputs
                elif size < EDGE:
                    term = padded[direction, line, pl.ds(EDGE + offset, line_len), :] * inputs
                elif offset > 0:
                    term = grad[size:] * inputs[: line_len - size]
                else:
                    term = grad[: line_len - size] * inputs[size:]
                sums[slot, :] += fold(term)
            return carry

        lax.fori_loop(0, lines, one_line, 0)

    def mix_line(direction, grad_mixed):
        parts[direction] = lax.dot_general(
            activated[direction], grad_mixed, (((0,), (0,)), ((), ())), preferred_element_type=F32
        ).astype(BF16)
        return [
            remote(
                parts.at[direction, rows(peer(step), piece)],
                a_recv.at[direction, step],
                a_send.at[direction, step],
                a_arrive.at[direction, step],
                {"line": peer(step)},
            )
            for step in range(1, ranks)
        ]

    def mix_dp(direction, copies_in):
        total = parts[direction, rows(me, piece), :].astype(F32)
        for step in range(1, ranks):
            copies_in[step - 1].wait_recv()
            total = total + a_recv[direction, step].astype(F32)
        b_recv[direction, my_dp] = total.astype(BF16)
        return [
            remote(
                b_recv.at[direction, my_dp],
                b_recv.at[direction, my_dp],
                b_send.at[direction, step],
                b_arrive.at[direction, step],
                {"dp": dp_peer(step)},
            )
            for step in range(1, copies)
        ]

    def mix_spread(direction, copies_in):
        for copy in copies_in:
            copy.wait_recv()
        total = b_recv[direction, 0].astype(F32)
        for index in range(1, copies):
            total = total + b_recv[direction, index].astype(F32)
        full[direction, rows(me, piece), :] = (total * scale).astype(BF16)
        return [
            remote(
                full.at[direction, rows(me, piece)],
                full.at[direction, rows(me, piece)],
                c_send.at[direction, step],
                c_arrive.at[direction, step],
                {"line": peer(step)},
            )
            for step in range(1, ranks)
        ]

    def mix_finish(direction, copies_in):
        for copy in copies_in:
            copy.wait_recv()
        mix_out[direction] = full[direction].astype(F32)

    def tail_line(direction):
        line_tails[direction, me] = jnp.sum(sums[...].reshape(taps + 1, 8, channels), axis=1)
        return [
            remote(
                line_tails.at[direction, me],
                line_tails.at[direction, me],
                t_send.at[direction, step],
                t_arrive.at[direction, step],
                {"line": peer(step)},
            )
            for step in range(1, ranks)
        ]

    def tail_dp(direction, copies_in):
        for copy in copies_in:
            copy.wait_recv()
        total = line_tails[direction, 0]
        for index in range(1, ranks):
            total = total + line_tails[direction, index]
        dp_tails[direction, my_dp] = total
        return [
            remote(
                dp_tails.at[direction, my_dp],
                dp_tails.at[direction, my_dp],
                u_send.at[direction, step],
                u_arrive.at[direction, step],
                {"dp": dp_peer(step)},
            )
            for step in range(1, copies)
        ]

    def tail_finish(direction, copies_in):
        for copy in copies_in:
            copy.wait_recv()
        total = dp_tails[direction, 0]
        for index in range(1, copies):
            total = total + dp_tails[direction, index]
        total = total * scale
        taps_out[direction] = total[:taps]
        gain_out[direction : direction + 1, :] = total[taps : taps + 1]

    moved = backward(2)
    arriving = hand_over(5, 2, moved, -1)
    a2 = mix_line(2, grads[...].astype(BF16))
    tap_sums(2)
    t2 = tail_line(2)
    grads[...] = take(5, 1, arriving)
    moved = backward(1)
    arriving = hand_over(6, 1, moved, -1)
    b2 = mix_dp(2, a2)
    a1 = mix_line(1, grads[...].astype(BF16))
    tap_sums(1)
    t1 = tail_line(1)
    u2 = tail_dp(2, t2)
    grads[...] = take(6, 0, arriving)
    a0 = mix_line(0, grads[...].astype(BF16))
    b1 = mix_dp(1, a1)
    moved = backward(0)
    b0 = mix_dp(0, a0)
    last_arriving, own_last = leave(7, 0, moved, field_grad)
    tap_sums(0)
    t0 = tail_line(0)
    c2 = mix_spread(2, b2)
    c1 = mix_spread(1, b1)
    u1 = tail_dp(1, t1)
    u0 = tail_dp(0, t0)
    c0 = mix_spread(0, b0)
    tail_finish(2, u2)
    mix_finish(2, c2)
    mix_finish(1, c1)
    tail_finish(1, u1)
    mix_finish(0, c0)
    tail_finish(0, u0)
    for copy in out_arriving + last_arriving:
        copy.wait_recv()
    own_out.wait()
    own_last.wait()
    for copy in unsent:
        copy.wait_send()


def write_out(*refs):
    count = (len(refs) - 2) // 3
    sources, targets, held = refs[:count], refs[count : 2 * count], refs[2 * count : 3 * count]
    in_sem, out_sem = refs[-2:]
    into = [
        pltpu.make_async_copy(sources[index], held[index], in_sem.at[index])
        for index in range(count)
    ]
    out = [
        pltpu.make_async_copy(held[index], targets[index], out_sem.at[index])
        for index in range(count)
    ]
    for move in into:
        move.start()
    for index in range(count):
        into[index].wait()
        out[index].start()
    for move in out:
        move.wait()


def body(fields, cotangent, norm_gain, kernel, mix_weight, line_order, line_starts):
    ranks = lax.axis_size("line")
    copies = lax.axis_size("dp")
    batch, cells, channels = fields.shape
    assert batch == 1
    directions, taps = kernel.shape[:2]
    lines = line_starts.shape[1]
    line_len = cells // lines
    scale = float(copies * batch * ranks * cells) ** (-0.5)
    piece = channels // ranks
    stages = 2 * directions + 2
    vmem = pl.BlockSpec(memory_space=pltpu.VMEM)
    hbm = pl.BlockSpec(memory_space=pltpu.HBM)
    anywhere = pl.BlockSpec(memory_space=pl.ANY)
    wide = pltpu.VMEM((directions, cells, channels), F32)
    edged = pltpu.VMEM((directions, lines, line_len + 2 * EDGE, channels), F32)
    dma = pltpu.SemaphoreType.DMA
    outs = (
        jax.ShapeDtypeStruct(fields.shape, BF16),
        jax.ShapeDtypeStruct(fields.shape, BF16),
        jax.ShapeDtypeStruct((directions, channels, channels), F32),
        jax.ShapeDtypeStruct((directions, taps, channels), F32),
        jax.ShapeDtypeStruct((directions, channels), F32),
    )
    results = pl.pallas_call(
        functools.partial(kernel_body, (ranks, copies, line_len, scale)),
        out_shape=outs,
        in_specs=[hbm] * 7,
        out_specs=(anywhere, anywhere, vmem, vmem, vmem),
        scratch_shapes=[
            pltpu.VMEM(norm_gain.shape, F32),
            pltpu.VMEM(kernel.shape, F32),
            pltpu.VMEM(mix_weight.shape, BF16),
            pltpu.VMEM(line_order.shape, jnp.int32),
            pltpu.VMEM(line_starts.shape, jnp.int32),
            pltpu.VMEM((directions, cells, cells), BF16),
            pltpu.VMEM((directions, cells, cells), BF16),
            pltpu.VMEM((stages, cells, channels), BF16),
            pltpu.VMEM((stages, cells, channels), BF16),
            pltpu.VMEM((cells, channels), F32),
            wide,
            wide,
            edged,
            wide,
            pltpu.VMEM((directions, cells, channels), BF16),
            pltpu.VMEM((cells, channels), F32),
            edged,
            pltpu.VMEM(((taps + 1) * 8, channels), F32),
            pltpu.VMEM((directions, channels, channels), BF16),
            pltpu.VMEM((directions, ranks, piece, channels), BF16),
            pltpu.VMEM((directions, copies, piece, channels), BF16),
            pltpu.VMEM((directions, channels, channels), BF16),
            pltpu.VMEM((directions, ranks, taps + 1, channels), F32),
            pltpu.VMEM((directions, copies, taps + 1, channels), F32),
            dma((stages, ranks)),
            dma((stages, ranks)),
            dma((directions, ranks)),
            dma((directions, ranks)),
            dma((directions, copies)),
            dma((directions, copies)),
            dma((directions, ranks)),
            dma((directions, ranks)),
            dma((directions, ranks)),
            dma((directions, ranks)),
            dma((directions, copies)),
            dma((directions, copies)),
            dma((stages,)),
            dma((5,)),
        ],
        compiler_params=pltpu.CompilerParams(
            collective_id=0, has_side_effects=True, vmem_limit_bytes=60 * 1024 * 1024
        ),
        name="mesh_block",
    )(fields, cotangent, norm_gain, kernel, mix_weight, line_order, line_starts)
    return pl.pallas_call(
        write_out,
        out_shape=outs,
        in_specs=[anywhere] * 5,
        out_specs=(hbm,) * 5,
        scratch_shapes=[pltpu.VMEM(out.shape, out.dtype) for out in outs] + [dma((5,)), dma((5,))],
        compiler_params=pltpu.CompilerParams(vmem_limit_bytes=60 * 1024 * 1024),
        name="write_out",
    )(*results)


def solution(mesh):
    in_specs = (
        P("dp", "line", None),
        P("dp", "line", None),
        P(),
        P(),
        P(),
        P(None, "line"),
        P(None, "line"),
    )
    out_specs = (P("dp", "line", None), P("dp", "line", None), P(), P(), P())
    return jax.shard_map(body, mesh=mesh, in_specs=in_specs, out_specs=out_specs, check_vma=False)
```

```python
import functools

import jax
import jax.numpy as jnp
from jax import lax
from jax.experimental import pallas as pl
from jax.experimental.pallas import tpu as pltpu
from jax.sharding import PartitionSpec as P

EPSILON = 1e-06
EDGE = 8
F32 = jnp.float32
BF16 = jnp.bfloat16


def tap_offsets(taps):
    offsets = [0]
    for dilation_level in range((taps - 1) // 2):
        offsets = offsets + [-(2**dilation_level), 2**dilation_level]
    return offsets


def fold(values):
    return jnp.sum(values.reshape(-1, 8, values.shape[1]), axis=0)


def kernel_body(
    shape,
    fields,
    cotangent,
    gain_hbm,
    taps_hbm,
    mix_hbm,
    order_hbm,
    starts_hbm,
    imitated,
    field_grad,
    mix_out,
    taps_out,
    gain_out,
    gain_ref,
    taps_ref,
    mix_ref,
    order_ref,
    starts_ref,
    gather,
    scatter,
    recv,
    placed,
    stream,
    scaled,
    inverse,
    masked,
    slope,
    activated,
    grads,
    padded,
    sums,
    parts,
    a_recv,
    b_recv,
    full,
    line_tails,
    dp_tails,
    ex_send,
    ex_recv,
    a_send,
    a_arrive,
    b_send,
    b_arrive,
    c_send,
    c_arrive,
    t_send,
    t_arrive,
    u_send,
    u_arrive,
    local_sem,
    load_sem,
):
    ranks, copies, line_len, scale = shape
    cells, channels = stream.shape
    lines = cells // line_len
    block = cells // ranks
    taps = taps_ref.shape[1]
    offsets = tap_offsets(taps)
    piece = parts.shape[1] // ranks
    me = lax.axis_index("line")
    my_dp = lax.axis_index("dp")

    loads = []
    for index, (source, target) in enumerate(
        (
            (order_hbm, order_ref),
            (gain_hbm, gain_ref),
            (taps_hbm, taps_ref),
            (starts_hbm, starts_ref),
            (mix_hbm, mix_ref),
        )
    ):
        load = pltpu.make_async_copy(source, target, load_sem.at[index])
        load.start()
        loads.append(load)

    def peer(step):
        return lax.rem(me + step, ranks)

    def dp_peer(step):
        return lax.rem(my_dp + step, copies)

    def rows(index, size):
        return pl.ds(pl.multiple_of(index * size, size), size)

    barrier = pltpu.get_barrier_semaphore()
    for step in range(1, ranks):
        pl.semaphore_signal(
            barrier, inc=1, device_id={"line": peer(step)}, device_id_type=pl.DeviceIdType.MESH
        )
    for step in range(1, copies):
        pl.semaphore_signal(
            barrier, inc=1, device_id={"dp": dp_peer(step)}, device_id_type=pl.DeviceIdType.MESH
        )
    pl.semaphore_wait(barrier, ranks - 1 + copies - 1)

    unsent = []

    def remote(source, target, send_sem, recv_sem, where):
        copy = pltpu.make_async_remote_copy(
            src_ref=source,
            dst_ref=target,
            send_sem=send_sem,
            recv_sem=recv_sem,
            device_id=where,
            device_id_type=pl.DeviceIdType.MESH,
        )
        copy.start()
        unsent.append(copy)
        return copy

    def send(stage, step, source, target):
        return remote(
            source, target, ex_send.at[stage, step], ex_recv.at[stage, step], {"line": peer(step)}
        )

    def enter(stage, array, shift):
        out = []
        for step in range(1, ranks):
            chunk = lax.rem(peer(step) + ranks * shift - shift * me, ranks)
            out.append(
                send(stage, step, array.at[0, rows(chunk, block)], recv.at[stage, rows(me, block)])
            )
        chunk = lax.rem(me + ranks * shift - shift * me, ranks)
        own = pltpu.make_async_copy(
            array.at[0, rows(chunk, block)], recv.at[stage, rows(me, block)], local_sem.at[stage]
        )
        own.start()
        return out, own

    arriving, own_fields = enter(0, fields, 0)

    def tables(direction):
        row = order_ref[direction : direction + 1, :]
        lanes = 128
        across = lax.broadcasted_iota(jnp.int32, (cells, cells), 0)
        scatter[direction] = jnp.where(across == row, 1.0, 0.0).astype(BF16)
        turned = jnp.transpose(jnp.broadcast_to(row, (lanes, cells)))
        for first in range(0, cells, lanes):
            width = lax.broadcasted_iota(jnp.int32, (cells, lanes), 1) + first
            gather[direction, :, first : first + lanes] = jnp.where(
                turned == width, 1.0, 0.0
            ).astype(BF16)

    masked[...] = jnp.zeros_like(masked)
    padded[...] = jnp.zeros_like(padded)
    for load in loads:
        load.wait()
    tables(0)

    def hand_over(stage, direction, values, sign):
        out = []
        for anchor in list(range(1, ranks)) + [0]:
            span = pl.ds(anchor * block, block)
            chunk = jnp.dot(
                scatter[direction, span, :], values, preferred_element_type=F32
            ).astype(BF16)
            if anchor:
                placed[stage, span, :] = chunk
                step = (sign * anchor) % ranks
                out.append(send(stage, step, placed.at[stage, span], recv.at[stage, span]))
            else:
                recv[stage, span, :] = chunk
        return out

    def leave(stage, direction, values, target):
        chunk = jnp.dot(scatter[direction], values, preferred_element_type=F32)
        placed[stage] = chunk.astype(BF16)
        out = []
        for step in range(1, ranks):
            anchor = peer(step)
            where = lax.rem(me + direction * (ranks - anchor), ranks)
            out.append(
                send(
                    stage,
                    step,
                    placed.at[stage, rows(anchor, block)],
                    target.at[0, rows(where, block)],
                )
            )
        where = lax.rem(me + direction * (ranks - me), ranks)
        own = pltpu.make_async_copy(
            placed.at[stage, rows(me, block)],
            target.at[0, rows(where, block)],
            local_sem.at[stage],
        )
        own.start()
        return out, own

    def take(stage, direction, copies_in):
        for copy in copies_in:
            copy.wait_recv()
        return jnp.dot(gather[direction], recv[stage], preferred_element_type=F32)

    def keep_rows(direction, line):
        position = lax.broadcasted_iota(jnp.int32, (line_len, channels), 0)
        return position >= starts_ref[direction : direction + 1, line : line + 1]

    inside = pl.ds(EDGE, line_len)

    def forward(direction):
        for line in range(lines):
            here = pl.ds(line * line_len, line_len)
            values = stream[here, :]
            norm = lax.rsqrt(jnp.mean(values * values, axis=-1, keepdims=True) + EPSILON)
            ratio = values * norm
            normed = (ratio * gain_ref[direction : direction + 1, :]).astype(BF16).astype(F32)
            masked[direction, line, inside, :] = jnp.where(keep_rows(direction, line), normed, 0.0)
            inverse[direction, here, :] = jnp.broadcast_to(norm, (line_len, channels))
            scaled[direction, here, :] = ratio

        def one_line(line, carry):
            here = rows(line, line_len)
            inputs = masked[direction, line, inside, :]
            hidden = taps_ref[direction, 0:1, :] * inputs
            for tap in range(1, taps):
                offset = offsets[tap]
                weight = taps_ref[direction, tap : tap + 1, :]
                size = abs(offset)
                if size < EDGE:
                    near = masked[direction, line, pl.ds(EDGE + offset, line_len), :]
                    hidden = hidden + weight * near
                elif offset > 0:
                    inner = hidden[: line_len - size] + weight * inputs[size:]
                    hidden = jnp.concatenate([inner, hidden[line_len - size :]], axis=0)
                else:
                    inner = hidden[size:] + weight * inputs[: line_len - size]
                    hidden = jnp.concatenate([hidden[:size], inner], axis=0)
            gate = 0.5 * jnp.tanh(0.5 * hidden) + 0.5
            activated[direction, here, :] = (hidden * gate).astype(BF16)
            slope[direction, here, :] = gate * (1.0 + hidden * (1.0 - gate))
            return carry

        lax.fori_loop(0, lines, one_line, 0, unroll=True)
        mixed = jnp.dot(activated[direction], mix_ref[direction], preferred_element_type=F32)
        return (stream[...] + mixed.astype(BF16).astype(F32)).astype(BF16)

    own_fields.wait()
    stream[...] = take(0, 0, arriving)
    cot_arriving, own_cot = enter(1, cotangent, 2)
    moved = forward(0)
    arriving = hand_over(2, 0, moved, 1)
    tables(1)
    stream[...] = take(2, 1, arriving)
    moved = forward(1)
    arriving = hand_over(3, 1, moved, 1)
    tables(2)
    stream[...] = take(3, 2, arriving)
    moved = forward(2)
    out_arriving, own_out = leave(4, 2, moved, imitated)
    own_cot.wait()
    grads[...] = take(1, 2, cot_arriving)

    def backward(direction):
        back = lax.dot_general(
            grads[...].astype(BF16),
            mix_ref[direction],
            (((1,), (1,)), ((), ())),
            preferred_element_type=F32,
        )
        for line in range(lines):
            here = pl.ds(line * line_len, line_len)
            local = back[line * line_len : (line + 1) * line_len] * slope[direction, here, :]
            padded[direction, line, inside, :] = local.astype(BF16).astype(F32)

        def one_line(line, carry):
            grad = padded[direction, line, inside, :]
            total = taps_ref[direction, 0:1, :] * grad
            for tap in range(1, taps):
                offset = -offsets[tap]
                weight = taps_ref[direction, tap : tap + 1, :]
                size = abs(offset)
                if size < EDGE:
                    near = padded[direction, line, pl.ds(EDGE + offset, line_len), :]
                    total = total + weight * near
                elif offset > 0:
                    inner = total[: line_len - size] + weight * grad[size:]
                    total = jnp.concatenate([inner, total[line_len - size :]], axis=0)
                else:
                    inner = total[size:] + weight * grad[: line_len - size]
                    total = jnp.concatenate([total[:size], inner], axis=0)
            stream[rows(line, line_len), :] = total
            return carry

        lax.fori_loop(0, lines, one_line, 0, unroll=True)
        out = []
        gains = jnp.zeros((8, channels), F32)
        for line in range(lines):
            here = pl.ds(line * line_len, line_len)
            total = jnp.where(keep_rows(direction, line), stream[here, :], 0.0)
            cell = total.astype(BF16).astype(F32)
            ratio = scaled[direction, here, :]
            gains = gains + fold(cell * ratio)
            weighted = cell * gain_ref[direction : direction + 1, :]
            centre = jnp.mean(weighted * ratio, axis=-1, keepdims=True)
            change = inverse[direction, here, :] * (weighted - ratio * centre)
            out.append((grads[here, :] + change).astype(BF16))
        sums[8 * taps : 8 * taps + 8, :] = gains
        return jnp.concatenate(out, axis=0)

    def tap_sums(direction):
        sums[0 : 8 * taps, :] = jnp.zeros((8 * taps, channels), F32)

        def one_line(line, carry):
            grad = padded[direction, line, inside, :]
            inputs = masked[direction, line, inside, :]
            for tap in range(taps):
                offset = -offsets[tap]
                size = abs(offset)
                slot = pl.ds(8 * tap, 8)
                if size == 0:
                    term = grad * inputs
                elif size < EDGE:
                    term = padded[direction, line, pl.ds(EDGE + offset, line_len), :] * inputs
                elif offset > 0:
                    term = grad[size:] * inputs[: line_len - size]
                else:
                    term = grad[: line_len - size] * inputs[size:]
                sums[slot, :] += fold(term)
            return carry

        lax.fori_loop(0, lines, one_line, 0)

    def mix_line(direction, grad_mixed):
        parts[direction] = lax.dot_general(
            activated[direction], grad_mixed, (((0,), (0,)), ((), ())), preferred_element_type=F32
        ).astype(BF16)
        return [
            remote(
                parts.at[direction, rows(peer(step), piece)],
                a_recv.at[direction, step],
                a_send.at[direction, step],
                a_arrive.at[direction, step],
                {"line": peer(step)},
            )
            for step in range(1, ranks)
        ]

    def mix_dp(direction, copies_in):
        total = parts[direction, rows(me, piece), :].astype(F32)
        for step in range(1, ranks):
            copies_in[step - 1].wait_recv()
            total = total + a_recv[direction, step].astype(F32)
        b_recv[direction, my_dp] = total.astype(BF16)
        return [
            remote(
                b_recv.at[direction, my_dp],
                b_recv.at[direction, my_dp],
                b_send.at[direction, step],
                b_arrive.at[direction, step],
                {"dp": dp_peer(step)},
            )
            for step in range(1, copies)
        ]

    def mix_spread(direction, copies_in):
        for copy in copies_in:
            copy.wait_recv()
        total = b_recv[direction, 0].astype(F32)
        for index in range(1, copies):
            total = total + b_recv[direction, index].astype(F32)
        full[direction, rows(me, piece), :] = (total * scale).astype(BF16)
        return [
            remote(
                full.at[direction, rows(me, piece)],
                full.at[direction, rows(me, piece)],
                c_send.at[direction, step],
                c_arrive.at[direction, step],
                {"line": peer(step)},
            )
            for step in range(1, ranks)
        ]

    def mix_finish(direction, copies_in):
        for copy in copies_in:
            copy.wait_recv()
        mix_out[direction] = full[direction].astype(F32)

    def tail_line(direction):
        line_tails[direction, me] = jnp.sum(sums[...].reshape(taps + 1, 8, channels), axis=1)
        return [
            remote(
                line_tails.at[direction, me],
                line_tails.at[direction, me],
                t_send.at[direction, step],
                t_arrive.at[direction, step],
                {"line": peer(step)},
            )
            for step in range(1, ranks)
        ]

    def tail_dp(direction, copies_in):
        for copy in copies_in:
            copy.wait_recv()
        total = line_tails[direction, 0]
        for index in range(1, ranks):
            total = total + line_tails[direction, index]
        dp_tails[direction, my_dp] = total
        return [
            remote(
                dp_tails.at[direction, my_dp],
                dp_tails.at[direction, my_dp],
                u_send.at[direction, step],
                u_arrive.at[direction, step],
                {"dp": dp_peer(step)},
            )
            for step in range(1, copies)
        ]

    def tail_finish(direction, copies_in):
        for copy in copies_in:
            copy.wait_recv()
        total = dp_tails[direction, 0]
        for index in range(1, copies):
            total = total + dp_tails[direction, index]
        total = total * scale
        taps_out[direction] = total[:taps]
        gain_out[direction : direction + 1, :] = total[taps : taps + 1]

    moved = backward(2)
    arriving = hand_over(5, 2, moved, -1)
    a2 = mix_line(2, grads[...].astype(BF16))
    tap_sums(2)
    t2 = tail_line(2)
    grads[...] = take(5, 1, arriving)
    moved = backward(1)
    arriving = hand_over(6, 1, moved, -1)
    b2 = mix_dp(2, a2)
    a1 = mix_line(1, grads[...].astype(BF16))
    tap_sums(1)
    t1 = tail_line(1)
    u2 = tail_dp(2, t2)
    grads[...] = take(6, 0, arriving)
    a0 = mix_line(0, grads[...].astype(BF16))
    b1 = mix_dp(1, a1)
    moved = backward(0)
    b0 = mix_dp(0, a0)
    last_arriving, own_last = leave(7, 0, moved, field_grad)
    tap_sums(0)
    t0 = tail_line(0)
    c2 = mix_spread(2, b2)
    c1 = mix_spread(1, b1)
    u1 = tail_dp(1, t1)
    u0 = tail_dp(0, t0)
    c0 = mix_spread(0, b0)
    tail_finish(2, u2)
    mix_finish(2, c2)
    mix_finish(1, c1)
    tail_finish(1, u1)
    mix_finish(0, c0)
    tail_finish(0, u0)
    for copy in out_arriving + last_arriving:
        copy.wait_recv()
    own_out.wait()
    own_last.wait()
    for copy in unsent:
        copy.wait_send()


def write_out(*refs):
    count = (len(refs) - 2) // 3
    sources, targets, held = refs[:count], refs[count : 2 * count], refs[2 * count : 3 * count]
    in_sem, out_sem = refs[-2:]
    into = [
        pltpu.make_async_copy(sources[index], held[index], in_sem.at[index])
        for index in range(count)
    ]
    out = [
        pltpu.make_async_copy(held[index], targets[index], out_sem.at[index])
        for index in range(count)
    ]
    for move in into:
        move.start()
    for index in range(count):
        into[index].wait()
        out[index].start()
    for move in out:
        move.wait()


def body(fields, cotangent, norm_gain, kernel, mix_weight, line_order, line_starts):
    ranks = lax.axis_size("line")
    copies = lax.axis_size("dp")
    batch, cells, channels = fields.shape
    assert batch == 1
    directions, taps = kernel.shape[:2]
    lines = line_starts.shape[1]
    line_len = cells // lines
    scale = float(copies * batch * ranks * cells) ** (-0.5)
    piece = channels // ranks
    stages = 2 * directions + 2
    vmem = pl.BlockSpec(memory_space=pltpu.VMEM)
    hbm = pl.BlockSpec(memory_space=pltpu.HBM)
    anywhere = pl.BlockSpec(memory_space=pl.ANY)
    wide = pltpu.VMEM((directions, cells, channels), F32)
    edged = pltpu.VMEM((directions, lines, line_len + 2 * EDGE, channels), F32)
    dma = pltpu.SemaphoreType.DMA
    outs = (
        jax.ShapeDtypeStruct(fields.shape, BF16),
        jax.ShapeDtypeStruct(fields.shape, BF16),
        jax.ShapeDtypeStruct((directions, channels, channels), F32),
        jax.ShapeDtypeStruct((directions, taps, channels), F32),
        jax.ShapeDtypeStruct((directions, channels), F32),
    )
    results = pl.pallas_call(
        functools.partial(kernel_body, (ranks, copies, line_len, scale)),
        out_shape=outs,
        in_specs=[hbm] * 7,
        out_specs=(anywhere, anywhere, vmem, vmem, vmem),
        scratch_shapes=[
            pltpu.VMEM(norm_gain.shape, F32),
            pltpu.VMEM(kernel.shape, F32),
            pltpu.VMEM(mix_weight.shape, BF16),
            pltpu.VMEM(line_order.shape, jnp.int32),
            pltpu.VMEM(line_starts.shape, jnp.int32),
            pltpu.VMEM((directions, cells, cells), BF16),
            pltpu.VMEM((directions, cells, cells), BF16),
            pltpu.VMEM((stages, cells, channels), BF16),
            pltpu.VMEM((stages, cells, channels), BF16),
            pltpu.VMEM((cells, channels), F32),
            wide,
            wide,
            edged,
            wide,
            pltpu.VMEM((directions, cells, channels), BF16),
            pltpu.VMEM((cells, channels), F32),
            edged,
            pltpu.VMEM(((taps + 1) * 8, channels), F32),
            pltpu.VMEM((directions, channels, channels), BF16),
            pltpu.VMEM((directions, ranks, piece, channels), BF16),
            pltpu.VMEM((directions, copies, piece, channels), BF16),
            pltpu.VMEM((directions, channels, channels), BF16),
            pltpu.VMEM((directions, ranks, taps + 1, channels), F32),
            pltpu.VMEM((directions, copies, taps + 1, channels), F32),
            dma((stages, ranks)),
            dma((stages, ranks)),
            dma((directions, ranks)),
            dma((directions, ranks)),
            dma((directions, copies)),
            dma((directions, copies)),
            dma((directions, ranks)),
            dma((directions, ranks)),
            dma((directions, ranks)),
            dma((directions, ranks)),
            dma((directions, copies)),
            dma((directions, copies)),
            dma((stages,)),
            dma((5,)),
        ],
        compiler_params=pltpu.CompilerParams(
            collective_id=0, has_side_effects=True, vmem_limit_bytes=60 * 1024 * 1024
        ),
        name="mesh_block",
    )(fields, cotangent, norm_gain, kernel, mix_weight, line_order, line_starts)
    return pl.pallas_call(
        write_out,
        out_shape=outs,
        in_specs=[anywhere] * 5,
        out_specs=(hbm,) * 5,
        scratch_shapes=[pltpu.VMEM(out.shape, out.dtype) for out in outs] + [dma((5,)), dma((5,))],
        compiler_params=pltpu.CompilerParams(vmem_limit_bytes=60 * 1024 * 1024),
        name="write_out",
    )(*results)


def solution(mesh):
    in_specs = (
        P("dp", "line", None),
        P("dp", "line", None),
        P(),
        P(),
        P(),
        P(None, "line"),
        P(None, "line"),
    )
    out_specs = (P("dp", "line", None), P("dp", "line", None), P(), P(), P())
    return jax.shard_map(body, mesh=mesh, in_specs=in_specs, out_specs=out_specs, check_vma=False)
```
